512 devices in a mesh: row: 16 (over x, y_lo, core), col: 32 (over z, y_hi).
Axes of the slice: x: 4, y: 8 (y_hi: 4, y_lo: 2; y = y_hi * 2 + y_lo), z: 8, core: 2. Of those that a mesh axis runs over, the one named last changes fastest.
Arguments:
- eigvecs: float32 [4096, 4096], P('row', 'col'), may hold values from -6 to 6
- offsets: int32 [1], replicated, may hold values from 0 to 127
- plan: int32 [1, 30], replicated, may hold values from 0 to 31
- refl_v: float32 [32, 255, 128], P('col')
- refl_t: float32 [32, 128, 128], P('col'), as said below
Outputs:
- updated: float32 [4096, 4096], P('row', 'col')
The draws below stay inside these ranges and needn't reach their ends.
Inputs may be any that keep to these rules, and one draw needn't show every extreme that they name: For each bank entry, I - refl_v refl_t refl_v^T is orthogonal up to rounding.
All inputs are finite; a program needn't handle non-finite values.
Results may differ from the reference program's by a relative error of at most 0.00015.
Values sent between devices are 32-bit elements; how exact they have to be, the bound alone decides.
A program may use at most 64 MiB of HBM per device.

```python
import jax
import jax.numpy as jnp
from jax import lax

NB = 128
SWEEPS = 1
ROWS = 4096
COLS = 4096
BANK = 32
BLOCKS = 30


HIGHEST = lax.Precision.HIGHEST


def build_factor(vectors):
    gram_matrix = jnp.dot(vectors.T, vectors, precision=HIGHEST)
    positions = jnp.arange(NB)

    def add_column(column, factor):
        house_scale = 2.0 / gram_matrix[column, column]
        correlation = jnp.where(positions < column, gram_matrix[:, column], 0.0)
        entries = -house_scale * jnp.dot(factor, correlation, precision=HIGHEST)
        entries = entries + house_scale * (positions == column).astype(jnp.float32)
        return factor.at[:, column].set(entries)
    return lax.fori_loop(0, NB, add_column, jnp.zeros((NB, NB), jnp.float32))


def make_bank(key):
    subkey = jax.random.fold_in(key, 7)
    row_ids = jnp.arange(2 * NB - 1)[:, None]
    col_ids = jnp.arange(NB)[None, :]
    inside = (row_ids > col_ids) & (row_ids < col_ids + NB)
    entries = 0.1 * jax.random.normal(subkey, (BANK, 2 * NB - 1, NB), jnp.float32)
    vectors = jnp.where(inside[None], entries, 0.0) + (row_ids == col_ids).astype(jnp.float32)[None]
    factors = lax.map(build_factor, vectors)
    return (vectors, factors)


def draw_refl_v(key, part):
    return make_bank(key)[0]


def draw_refl_t(key, part):
    return make_bank(key)[1]


def touch_ends(values, own_key, least, top_value):
    longest = values.shape.index(max(values.shape))
    spots = []
    for shift in (0, 1):
        where = [jax.random.randint(jax.random.fold_in(own_key, axis), (), 0, length) for axis, length in enumerate(values.shape)]
        where[longest] = (where[longest] + shift) % values.shape[longest]
        spots.append(tuple(where))
    return values.at[spots[0]].set(least).at[spots[1]].set(top_value)


def block_scale(rng, extent, shards, low, top_value):
    def one(axis_at, shards_of):
        steps = jax.random.uniform(jax.random.fold_in(jax.random.fold_in(rng, 6), axis_at), (shards_of,), jnp.float32, low / len(shards), top_value / len(shards))
        return jnp.repeat(jnp.exp(steps), extent[axis_at] // shards_of).reshape((-1,) + (1,) * (len(extent) - axis_at - 1))

    gain = one(*shards[0])
    for cut in shards[1:]:
        gain = gain * one(*cut)
    return gain


def scatter_about(key, dims, width, most, shards=(), dtype=jnp.bfloat16):
    factor_of = block_scale(key, dims, shards, -0.22, 0.18) if shards else 1.0
    values = jax.random.normal(key, dims, jnp.float32) * width * factor_of
    return jnp.minimum(jnp.maximum(values, -most), most).astype(dtype)


def setup_inputs(seed: int = 0) -> dict:
    key_list = jax.random.split(jax.random.key(seed), 6)
    eigvecs = scatter_about(key_list[0], (ROWS, COLS), 1.0, 6.0, ((0, 16), (1, 32)), jnp.float32)
    offsets = jax.random.randint(key_list[1], (SWEEPS,), 0, NB).astype(jnp.int32)
    plan = touch_ends(jax.random.randint(key_list[2], (SWEEPS, BLOCKS), 0, BANK), jax.random.fold_in(key_list[2], 1), 0, BANK - 1).astype(jnp.int32)
    refl_v = draw_refl_v(jax.random.fold_in(key_list[5], 71), 0)
    refl_t = draw_refl_t(jax.random.fold_in(key_list[5], 71), 0)
    return {"eigvecs": eigvecs, "offsets": offsets, "plan": plan, "refl_v": refl_v, "refl_t": refl_t}


HIGHEST = lax.Precision.HIGHEST


def reference(eigvecs, offsets, plan, refl_v, refl_t):
    matrix = eigvecs
    for sweep in range(SWEEPS):
        first_row = offsets[sweep].astype(jnp.int32)

        def apply_block(index, matrix):
            index = jnp.asarray(index).astype(jnp.int32)
            row_start = (first_row + index * NB).astype(jnp.int32)
            block_rows = lax.dynamic_slice_in_dim(matrix, row_start, 2 * NB - 1, 0)
            block_id = plan[sweep, index]
            vectors = refl_v[block_id]
            factor = refl_t[block_id]
            inner_prod = jnp.dot(vectors.T, block_rows, precision=HIGHEST)
            scaled = jnp.dot(factor, inner_prod, precision=HIGHEST)
            block_rows = block_rows - jnp.dot(vectors, scaled, precision=HIGHEST)
            return lax.dynamic_update_slice_in_dim(matrix, block_rows, row_start, 0)

        matrix = lax.fori_loop(0, BLOCKS, apply_block, matrix)
    return matrix
```

```python
import functools

import jax
import jax.numpy as jnp
from jax import lax
from jax.experimental import pallas as pl
from jax.experimental.pallas import tpu as pltpu
from jax.sharding import PartitionSpec as P

MESH = pl.DeviceIdType.MESH
F32 = jnp.float32
BF16 = jnp.bfloat16


def split(a):
    hi = a.astype(BF16)
    return hi, (a - hi.astype(F32)).astype(BF16)


def mm(a, b, rhs_t=False):
    dims = (((1,), (1 if rhs_t else 0,)), ((), ()))
    ah, al = split(a)
    bh, bl = split(b)
    dot = functools.partial(
        lax.dot_general, dimension_numbers=dims, preferred_element_type=F32
    )
    return dot(ah, bl) + dot(al, bh) + dot(ah, bh)


def both(pair):
    return jnp.concatenate([pair[0], pair[1]], axis=1)


def far_first(cols):
    inner = 4 if cols % 4 == 0 else 1
    outer = cols // inner
    found = []
    for dz in range(outer):
        for dy in range(inner):
            if dz or dy:
                found.append((min(dz, outer - dz) + 2 * min(dy, inner - dy), dz, dy))
    found.sort(reverse=True)
    return inner, outer, [(dz, dy) for _, dz, dy in found]


def kernel(
    rows, cols, off_ref, plan_ref, e_ref, v_ref, t_ref, y_ref,
    xin, vbuf, tbuf, mine, g1, stage, g2, ebuf, p1buf, fbuf, abuf, hbuf, bbuf, sbuf, smbuf, srecv, cbuf, dbuf,
    lsem, hsem, s1, s2, psem, asem, bsend, brecv, dsem,
):
    nb = t_ref.shape[1]
    part = nb // rows
    own = e_ref.shape[0]
    r = lax.axis_index("row")
    c = lax.axis_index("col")
    core, pair, x = r % 2, (r // 2) % 2, r // 4
    groups = rows // 4
    inner, outer, spread = far_first(cols)
    blocks = 2 * rows - 2

    def col_at(dz, dy):
        return lax.rem(c // inner + dz, outer) * inner + lax.rem(c % inner + dy, inner)

    def row_at(k):
        return lax.rem(r + k, rows)

    def remote(src, dst, send, recv, to_row, to_col):
        return pltpu.make_async_remote_copy(
            src_ref=src, dst_ref=dst, send_sem=send, recv_sem=recv,
            device_id=(to_row, to_col), device_id_type=MESH,
        )

    barrier = pltpu.get_barrier_semaphore()
    for dz, dy in spread:
        pl.semaphore_signal(barrier, 1, device_id=(r, col_at(dz, dy)), device_id_type=MESH)
    for k in range(1, rows):
        pl.semaphore_signal(barrier, 1, device_id=(row_at(k), c), device_id_type=MESH)

    vbuf[2 * nb - 1 : 2 * nb] = jnp.zeros((1, nb), F32)
    xin[0:nb] = jnp.zeros((nb, nb), F32)
    get_v = pltpu.make_async_copy(v_ref.at[0], vbuf.at[pl.ds(0, 2 * nb - 1)], lsem.at[0])
    get_t = pltpu.make_async_copy(t_ref.at[0], tbuf, lsem.at[1])
    get_e = pltpu.make_async_copy(e_ref, xin.at[pl.ds(nb, own)], lsem.at[2])
    get_v.start()
    get_t.start()
    get_e.start()
    get_v.wait()
    get_t.wait()
    at = pl.multiple_of(r * part, part)
    row_ids = lax.broadcasted_iota(jnp.int32, (part, nb), 0) + at
    col_ids = lax.broadcasted_iota(jnp.int32, (part, nb), 1)
    mine[0:part] = jnp.where(
        row_ids >= col_ids, vbuf[pl.ds(at, part)], vbuf[pl.ds(nb + at, part)]
    )
    mine[part : 2 * part] = tbuf[pl.ds(at, part)]
    g1[c] = mine[...]

    pl.semaphore_wait(barrier, cols - 1 + rows - 1)

    for dz, dy in spread:
        remote(mine, g1.at[c], s1.at[0], s1.at[1], r, col_at(dz, dy)).start()
    head = remote(
        e_ref, xin.at[pl.ds(nb + own, own)], hsem.at[0], hsem.at[1], row_at(rows - 1), c
    )
    head.start()
    got1 = g1.at[pl.ds(0, cols - 1)]
    pltpu.make_async_copy(got1, got1, s1.at[1]).wait()

    order = sorted(range(1, rows), key=lambda k: -min(k, rows - k)) + [0]
    for k in order:
        to = row_at(k)
        for j in range(3):
            block = jnp.clip(2 * to - 1 + j, 0, blocks - 1)
            picked = g1[plan_ref[0, block]]
            if k:
                stage[k, 2 * part * j : 2 * part * (j + 1)] = picked
            else:
                g2[r, 2 * part * j : 2 * part * (j + 1)] = picked
        if k:
            remote(stage.at[k], g2.at[r], s2.at[0], s2.at[1], to, c).start()

    get_e.wait()
    head.wait_recv()
    off = off_ref[0]
    s0 = xin[pl.ds(off, nb)]
    fresh = [xin[pl.ds(off + nb * (1 + j), nb)] for j in range(3)]

    got2 = g2.at[pl.ds(0, rows - 1)]
    pltpu.make_async_copy(got2, got2, s2.at[1]).wait()

    ri = lax.broadcasted_iota(jnp.int32, (nb, nb), 0)
    ci = lax.broadcasted_iota(jnp.int32, (nb, nb), 1)
    eye = (ri == ci).astype(F32)
    maps = []
    for j in range(3):
        number = 2 * r - 1 + j
        live = ((number >= 0) & (number < blocks)).astype(F32)
        lo = 2 * part * j
        packed = g2[:, lo : lo + part].reshape(nb, nb)
        factor = g2[:, lo + part : lo + 2 * part].reshape(nb, nb) * live
        lower = jnp.where(ri >= ci, packed, 0.0)
        upper = jnp.where(ri >= ci, 0.0, packed)
        vectors = jnp.concatenate([lower, upper], axis=0)
        tv = mm(factor, vectors, rhs_t=True)
        m, n = tv[:, :nb], tv[:, nb:]
        z = mm(n, fresh[j])
        w = mm(vectors, jnp.concatenate([m, z], axis=1))
        maps.append((eye - w[:nb, :nb], -w[:nb, nb:], -w[nb:, :nb], fresh[j] - w[nb:, nb:]))
    (c0, d0, a0, b0), (c1, d1, a1, b1), (c2, d2, a2, b2) = maps
    w = mm(jnp.concatenate([c1, a1], axis=0), jnp.concatenate([a0, b0], axis=1))
    cbuf[0:nb] = c0
    dbuf[0:nb] = d0
    cbuf[nb : 2 * nb] = w[:nb, :nb]
    dbuf[nb : 2 * nb] = w[:nb, nb:] + d1
    ebuf[0] = w[nb:, :nb]
    ebuf[1] = w[nb:, nb:] + b1

    to_core1 = remote(ebuf, p1buf, psem.at[0], psem.at[1], r ^ 1, c)
    to_pair = remote(fbuf, abuf, asem.at[0], asem.at[1], r ^ 2, c)
    to_core0 = remote(smbuf, srecv, dsem.at[0], dsem.at[1], r ^ 1, c)

    @pl.when(core == 0)
    def _():
        to_core1.start()

    w = mm(c2, both(ebuf))
    cbuf[2 * nb : 3 * nb] = w[:, :nb]
    dbuf[2 * nb : 3 * nb] = w[:, nb:] + d2

    def along_x(step, half):
        return remote(
            hbuf.at[half], bbuf.at[x, half], bsend.at[step, half], brecv.at[x, half],
            lax.rem(r + 4 * step, rows), c,
        )

    def from_x(source, half):
        slot = bbuf.at[source, half]
        return pltpu.make_async_copy(slot, slot, brecv.at[source, half])

    @pl.when(core == 1)
    def _():
        to_core1.wait_recv()
        w = mm(ebuf[0], both(p1buf))
        fbuf[0] = w[:, :nb]
        fbuf[1] = w[:, nb:] + ebuf[1]
        to_pair.start()
        to_pair.wait_recv()
        first = pair == 0
        late_g = jnp.where(first, abuf[0], fbuf[0])
        late_b = jnp.where(first, abuf[1], fbuf[1])
        early = jnp.where(first, both(fbuf), both(abuf))
        w = mm(late_g, early)
        hbuf[0] = w[:, :nb]
        hbuf[1] = w[:, nb:] + late_b
        for step in range(1, groups):
            @pl.when(x + step < groups)
            def _(step=step):
                along_x(step, 1).start()

                @pl.when(x > 0)
                def _():
                    along_x(step, 0).start()

        @pl.when(x == 0)
        def _():
            sbuf[...] = s0

        for source in range(groups - 1):
            @pl.when(x > source)
            def _(source=source):
                from_x(source, 1).wait()
                if source:
                    from_x(source, 0).wait()
                    sbuf[...] = mm(bbuf[source, 0], sbuf[...]) + bbuf[source, 1]
                else:
                    sbuf[...] = bbuf[source, 1]

        @pl.when(pair == 0)
        def _():
            smbuf[...] = sbuf[...]

        @pl.when(pair == 1)
        def _():
            smbuf[...] = mm(abuf[0], sbuf[...]) + abuf[1]

        to_core0.start()
        sbuf[...] = mm(p1buf[0], smbuf[...]) + p1buf[1]

    @pl.when(core == 0)
    def _():
        to_core0.wait_recv()
        sbuf[...] = jnp.where(r == 0, s0, srecv[...])

    y_ref[...] = mm(cbuf[...], sbuf[...]) + dbuf[...]

    pltpu.make_async_copy(got1, got1, s1.at[0]).wait()
    pltpu.make_async_copy(got2, got2, s2.at[0]).wait()
    head.wait_send()

    @pl.when(core == 0)
    def _():
        to_core1.wait_send()

    @pl.when(core == 1)
    def _():
        to_pair.wait_send()
        to_core0.wait_send()
        for step in range(1, groups):
            @pl.when(x + step < groups)
            def _(step=step):
                along_x(step, 1).wait_send()

                @pl.when(x > 0)
                def _():
                    along_x(step, 0).wait_send()


def solution(mesh):
    rows, cols = mesh.shape["row"], mesh.shape["col"]

    def on_device(eigvecs, offsets, plan, refl_v, refl_t):
        own, width = eigvecs.shape
        nb = refl_t.shape[1]
        part = nb // rows
        dma = pltpu.SemaphoreType.DMA
        square = (nb, nb)
        y = pl.pallas_call(
            functools.partial(kernel, rows, cols),
            out_shape=jax.ShapeDtypeStruct((3 * nb, width), F32),
            in_specs=[
                pl.BlockSpec(memory_space=pltpu.SMEM),
                pl.BlockSpec(memory_space=pltpu.SMEM),
                pl.BlockSpec(memory_space=pl.ANY),
                pl.BlockSpec(memory_space=pl.ANY),
                pl.BlockSpec(memory_space=pl.ANY),
            ],
            out_specs=pl.BlockSpec(memory_space=pltpu.VMEM),
            scratch_shapes=[
                pltpu.VMEM((nb + 2 * own, width), F32),
                pltpu.VMEM((2 * nb, nb), F32),
                pltpu.VMEM(square, F32),
                pltpu.VMEM((2 * part, nb), F32),
                pltpu.VMEM((cols, 2 * part, nb), F32),
                pltpu.VMEM((rows, 6 * part, nb), F32),
                pltpu.VMEM((rows, 6 * part, nb), F32),
                pltpu.VMEM((2,) + square, F32),
                pltpu.VMEM((2,) + square, F32),
                pltpu.VMEM((2,) + square, F32),
                pltpu.VMEM((2,) + square, F32),
                pltpu.VMEM((2,) + square, F32),
                pltpu.VMEM((rows // 4, 2) + square, F32),
                pltpu.VMEM(square, F32),
                pltpu.VMEM(square, F32),
                pltpu.VMEM(square, F32),
                pltpu.VMEM((3 * nb, nb), F32),
                pltpu.VMEM((3 * nb, width), F32),
                dma((3,)), dma((2,)), dma((2,)), dma((2,)), dma((2,)), dma((2,)),
                dma((rows // 4, 2)), dma((rows // 4, 2)), dma((2,)),
            ],
            compiler_params=pltpu.CompilerParams(
                collective_id=0, has_side_effects=True, vmem_limit_bytes=24 * 2**20
            ),
            cost_estimate=pl.CostEstimate(
                flops=2 * 30 * nb**3, bytes_accessed=4 * 10 * nb * nb, transcendentals=0
            ),
            name="chase",
        )(offsets, plan, eigvecs, refl_v, refl_t)
        return lax.dynamic_slice(y, (nb - offsets[0], 0), (own, width))

    return jax.shard_map(
        on_device,
        mesh=mesh,
        in_specs=(P("row", "col"), P(), P(), P("col", None, None), P("col", None, None)),
        out_specs=P("row", "col"),
        check_vma=False,
    )
```

```python
import functools

import jax
import jax.numpy as jnp
from jax import lax
from jax.experimental import pallas as pl
from jax.experimental.pallas import tpu as pltpu
from jax.sharding import PartitionSpec as P

MESH = pl.DeviceIdType.MESH
F32 = jnp.float32
BF16 = jnp.bfloat16


def split(a):
    hi = a.astype(BF16)
    return hi, (a - hi.astype(F32)).astype(BF16)


def mm(a, b, rhs_t=False):
    dims = (((1,), (1 if rhs_t else 0,)), ((), ()))
    ah, al = split(a)
    bh, bl = split(b)
    dot = functools.partial(
        lax.dot_general, dimension_numbers=dims, preferred_element_type=F32
    )
    return dot(ah, bl) + dot(al, bh) + dot(ah, bh)


def both(pair):
    return jnp.concatenate([pair[0], pair[1]], axis=1)


def classes(cols):
    if cols == 32:
        start_z = (0.0, 0.9, 1.9, 2.8, 5.8, 6.7, 7.6, 8.4)
        start_y = (0.4, 2.2, 4.7, 3.3)
        start = {4 * z + y: start_z[z] + start_y[y] for z in range(8) for y in range(4)}
        served = {(7, 0): (6, 0), (5, 1): (4, 1), (6, 1): (5, 0), (7, 1): (0, 1)}
        for y in (2, 3):
            served.update({(4 + k, y): (3 - k, y) for k in range(4)})
        partner = {4 * a + b: 4 * d + e for (a, b), (d, e) in served.items()}
    else:
        start = {k: k for k in range(cols)}
        partner = {k: k - cols // 2 for k in range((cols + 1) // 2, cols)}
    order = sorted(start, key=lambda k: start[k])
    return [k for k in order if k not in partner], partner


def kernel(
    rows, cols, off_ref, plan_ref, e_ref, v_ref, t_ref, y_ref,
    xin, vbuf, tbuf, mine, g1, stage, stage3, g2, g3, ebuf, p1buf, fbuf, abuf, hbuf, bbuf, pbuf, sbuf, cbuf, dbuf,
    lsem, hsem, s1, s2, s3, psem, asem, bsend, brecv, dsem, qsem, rowsem,
):
    nb = t_ref.shape[1]
    part = nb // rows
    own = e_ref.shape[0]
    r = lax.axis_index("row")
    c = lax.axis_index("col")
    core, pair, x = r % 2, (r // 2) % 2, r // 4
    groups = rows // 4
    early, partner = classes(cols)
    blocks = 2 * rows - 2

    is_late = functools.reduce(jnp.logical_or, [c == k for k in partner])
    serves = functools.reduce(jnp.logical_or, [c == k for k in partner.values()])
    other = sum(
        jnp.where(c == a, b, 0) + jnp.where(c == b, a, 0) for a, b in partner.items()
    )
    is_early = jnp.logical_not(is_late)

    def row_at(k):
        return lax.rem(r + k, rows)

    def remote(src, dst, send, recv, to_row, to_col):
        return pltpu.make_async_remote_copy(
            src_ref=src, dst_ref=dst, send_sem=send, recv_sem=recv,
            device_id=(to_row, to_col), device_id_type=MESH,
        )

    def signal(sem, to_row, to_col):
        pl.semaphore_signal(sem, 1, device_id=(to_row, to_col), device_id_type=MESH)

    def await_bytes(ref, sem):
        pltpu.make_async_copy(ref, ref, sem).wait()

    vbuf[2 * nb - 1 : 2 * nb] = jnp.zeros((1, nb), F32)
    get_v = pltpu.make_async_copy(v_ref.at[0], vbuf.at[pl.ds(0, 2 * nb - 1)], lsem.at[0])
    get_t = pltpu.make_async_copy(t_ref.at[0], tbuf, lsem.at[1])
    get_e = pltpu.make_async_copy(e_ref, xin.at[pl.ds(nb, own)], lsem.at[2])
    get_v.start()
    get_t.start()
    get_e.start()

    barrier = pltpu.get_barrier_semaphore()

    @pl.when(is_early)
    def _():
        for k in list(partner) + early[::-1]:
            @pl.when(c != k)
            def _(k=k):
                signal(barrier, r, k)
        for k in range(1, rows):
            signal(barrier, row_at(k), c)

        @pl.when(serves)
        def _():
            for k in range(1, rows):
                signal(barrier, row_at(k), other)

    xin[0:nb] = jnp.zeros((nb, nb), F32)
    get_v.wait()
    get_t.wait()
    at = pl.multiple_of(r * part, part)
    row_ids = lax.broadcasted_iota(jnp.int32, (part, nb), 0) + at
    col_ids = lax.broadcasted_iota(jnp.int32, (part, nb), 1)
    mine[0:part] = jnp.where(
        row_ids >= col_ids, vbuf[pl.ds(at, part)], vbuf[pl.ds(nb + at, part)]
    )
    mine[part : 2 * part] = tbuf[pl.ds(at, part)]

    pl.semaphore_wait(barrier, len(early) + rows - 1 - is_early.astype(jnp.int32))

    for k in early:
        @pl.when(c != k)
        def _(k=k):
            remote(mine, g1.at[c], s1.at[0], s1.at[1], r, k).start()

    head = remote(
        e_ref, xin.at[pl.ds(nb + own, own)], hsem.at[0], hsem.at[1], row_at(rows - 1), c
    )

    @pl.when(is_early)
    def _():
        head.start()
        g1[c] = mine[...]
        await_bytes(g1.at[pl.ds(0, cols - 1)], s1.at[1])

    @pl.when(is_late)
    def _():
        for k in range(1, rows):
            signal(rowsem, row_at(k), other)
        await_bytes(g1, s1.at[1])
        head.start()

    order = sorted(range(1, rows), key=lambda k: -min(k, rows - k)) + [0]

    def pick(to, j):
        return g1[plan_ref[0, jnp.clip(2 * to - 1 + j, 0, blocks - 1)]]

    for k in order:
        to = row_at(k)
        dst = stage.at[k] if k else g2.at[r]
        dst[0 : 2 * part] = pick(to, 0)
        dst[2 * part : 4 * part] = pick(to, 1)
        if k:
            remote(stage.at[k], g2.at[r], s2.at[0], s2.at[1], to, c).start()

    relay = remote(g1, g1, qsem.at[0], s1.at[1], r, other)

    @pl.when(serves)
    def _():
        pl.semaphore_wait(rowsem, rows - 1)
        relay.start()

    for k in order:
        to = row_at(k)
        dst = stage3.at[k] if k else g3.at[r]
        dst[...] = pick(to, 2)
        if k:
            remote(stage3.at[k], g3.at[r], s3.at[0], s3.at[1], to, c).start()

    get_e.wait()
    head.wait_recv()
    off = off_ref[0]
    s0 = xin[pl.ds(off, nb)]

    ri = lax.broadcasted_iota(jnp.int32, (nb, nb), 0)
    ci = lax.broadcasted_iota(jnp.int32, (nb, nb), 1)
    eye = (ri == ci).astype(F32)

    def block_map(j, packed, factor):
        number = 2 * r - 1 + j
        live = ((number >= 0) & (number < blocks)).astype(F32)
        fresh = xin[pl.ds(off + nb * (1 + j), nb)]
        packed = packed.reshape(nb, nb)
        factor = factor.reshape(nb, nb) * live
        lower = jnp.where(ri >= ci, packed, 0.0)
        upper = jnp.where(ri >= ci, 0.0, packed)
        vectors = jnp.concatenate([lower, upper], axis=0)
        tv = mm(factor, vectors, rhs_t=True)
        m, n = tv[:, :nb], tv[:, nb:]
        z = mm(n, fresh)
        w = mm(vectors if j < 2 else lower, jnp.concatenate([m, z], axis=1))
        if j == 2:
            return eye - w[:, :nb], -w[:, nb:]
        return eye - w[:nb, :nb], -w[:nb, nb:], -w[nb:, :nb], fresh - w[nb:, nb:]

    await_bytes(g2.at[pl.ds(0, rows - 1)], s2.at[1])
    c0, d0, a0, b0 = block_map(0, g2[:, 0:part], g2[:, part : 2 * part])
    c1, d1, a1, b1 = block_map(1, g2[:, 2 * part : 3 * part], g2[:, 3 * part : 4 * part])
    w = mm(jnp.concatenate([a1, c1], axis=0), jnp.concatenate([a0, b0], axis=1))
    ebuf[0] = w[:nb, :nb]
    ebuf[1] = w[:nb, nb:] + b1

    to_core1 = remote(ebuf, p1buf, psem.at[0], psem.at[1], r ^ 1, c)
    to_pair = remote(fbuf, abuf, asem.at[0], asem.at[1], r ^ 2, c)
    prefix = remote(abuf, pbuf, psem.at[0], psem.at[1], r ^ 1, c)
    state = remote(sbuf, sbuf, dsem.at[0], dsem.at[1], r ^ 1, c)
    core0, core1 = core == 0, core == 1

    @pl.when(core0)
    def _():
        to_core1.start()

    cbuf[0:nb] = c0
    dbuf[0:nb] = d0
    cbuf[nb : 2 * nb] = w[nb:, :nb]
    dbuf[nb : 2 * nb] = w[nb:, nb:] + d1

    @pl.when(core1)
    def _():
        to_core1.wait_recv()
        w = mm(ebuf[0], both(p1buf))
        fbuf[0] = w[:, :nb]
        fbuf[1] = w[:, nb:] + ebuf[1]
        to_pair.start()

    await_bytes(g3.at[pl.ds(0, rows - 1)], s3.at[1])
    c2, d2 = block_map(2, g3[:, 0:part], g3[:, part : 2 * part])
    w = mm(c2, both(ebuf))
    cbuf[2 * nb : 3 * nb] = w[:, :nb]
    dbuf[2 * nb : 3 * nb] = w[:, nb:] + d2

    def along_x(step, half):
        return remote(
            hbuf.at[half], bbuf.at[x, half], bsend.at[step, half], brecv.at[x, half],
            lax.rem(r + 4 * step, rows), c,
        )

    @pl.when(core1)
    def _():
        to_pair.wait_recv()
        first = pair == 0

        @pl.when(pair == 1)
        def _():
            prefix.start()

        late_g = jnp.where(first, abuf[0], fbuf[0])
        late_b = jnp.where(first, abuf[1], fbuf[1])
        early_pair = jnp.where(first, both(fbuf), both(abuf))
        w = mm(late_g, early_pair)
        hbuf[0] = w[:, :nb]
        hbuf[1] = w[:, nb:] + late_b
        for step in range(1, groups):
            @pl.when(x + step < groups)
            def _(step=step):
                along_x(step, 1).start()

                @pl.when(x > 0)
                def _():
                    along_x(step, 0).start()

        @pl.when(pair == 0)
        def _():
            pbuf[...] = p1buf[...]

        @pl.when(pair == 1)
        def _():
            w = mm(p1buf[0], both(abuf))
            pbuf[0] = w[:, :nb]
            pbuf[1] = w[:, nb:] + p1buf[1]

    @pl.when(core0 & (pair == 1))
    def _():
        prefix.wait_recv()

    @pl.when(core1 | (pair == 1))
    def _():
        w = mm(cbuf[...], both(pbuf))
        cbuf[...] = w[:, :nb]
        dbuf[...] = w[:, nb:] + dbuf[...]

    @pl.when(x == 0)
    def _():
        sbuf[...] = s0

    @pl.when((x > 0) & core1)
    def _():
        for source in range(groups - 1):
            @pl.when(x > source)
            def _(source=source):
                await_bytes(bbuf.at[source, 1], brecv.at[source, 1])
                if source:
                    await_bytes(bbuf.at[source, 0], brecv.at[source, 0])
                    sbuf[...] = mm(bbuf[source, 0], sbuf[...]) + bbuf[source, 1]
                else:
                    sbuf[...] = bbuf[source, 1]
        state.start()

    @pl.when((x > 0) & core0)
    def _():
        state.wait_recv()

    y_ref[...] = mm(cbuf[...], sbuf[...]) + dbuf[...]

    sent = g1.at[pl.ds(0, len(early) - 1)]
    await_bytes(sent, s1.at[0])
    head.wait_send()
    await_bytes(g2.at[pl.ds(0, rows - 1)], s2.at[0])
    await_bytes(g3.at[pl.ds(0, rows - 1)], s3.at[0])

    @pl.when(is_late)
    def _():
        await_bytes(g1.at[0], s1.at[0])

    @pl.when(serves)
    def _():
        relay.wait_send()

    @pl.when(core0)
    def _():
        to_core1.wait_send()

    @pl.when(core1)
    def _():
        to_pair.wait_send()

        @pl.when(pair == 1)
        def _():
            prefix.wait_send()

        @pl.when(x > 0)
        def _():
            state.wait_send()

        for step in range(1, groups):
            @pl.when(x + step < groups)
            def _(step=step):
                along_x(step, 1).wait_send()

                @pl.when(x > 0)
                def _():
                    along_x(step, 0).wait_send()


def solution(mesh):
    rows, cols = mesh.shape["row"], mesh.shape["col"]

    def on_device(eigvecs, offsets, plan, refl_v, refl_t):
        own, width = eigvecs.shape
        nb = refl_t.shape[1]
        part = nb // rows
        dma = pltpu.SemaphoreType.DMA
        square = (nb, nb)
        y = pl.pallas_call(
            functools.partial(kernel, rows, cols),
            out_shape=jax.ShapeDtypeStruct((3 * nb, width), F32),
            in_specs=[
                pl.BlockSpec(memory_space=pltpu.SMEM),
                pl.BlockSpec(memory_space=pltpu.SMEM),
                pl.BlockSpec(memory_space=pltpu.HBM),
                pl.BlockSpec(memory_space=pltpu.HBM),
                pl.BlockSpec(memory_space=pltpu.HBM),
            ],
            out_specs=pl.BlockSpec(memory_space=pltpu.VMEM),
            scratch_shapes=[
                pltpu.VMEM((nb + 2 * own, width), F32),
                pltpu.VMEM((2 * nb, nb), F32),
                pltpu.VMEM(square, F32),
                pltpu.VMEM((2 * part, nb), F32),
                pltpu.VMEM((cols, 2 * part, nb), F32),
                pltpu.VMEM((rows, 4 * part, nb), F32),
                pltpu.VMEM((rows, 2 * part, nb), F32),
                pltpu.VMEM((rows, 4 * part, nb), F32),
                pltpu.VMEM((rows, 2 * part, nb), F32),
                pltpu.VMEM((2,) + square, F32),
                pltpu.VMEM((2,) + square, F32),
                pltpu.VMEM((2,) + square, F32),
                pltpu.VMEM((2,) + square, F32),
                pltpu.VMEM((2,) + square, F32),
                pltpu.VMEM((rows // 4, 2) + square, F32),
                pltpu.VMEM((2,) + square, F32),
                pltpu.VMEM(square, F32),
                pltpu.VMEM((3 * nb, nb), F32),
                pltpu.VMEM((3 * nb, width), F32),
                dma((3,)), dma((2,)), dma((2,)), dma((2,)), dma((2,)), dma((2,)), dma((2,)),
                dma((rows // 4, 2)), dma((rows // 4, 2)), dma((2,)), dma((1,)),
                pltpu.SemaphoreType.REGULAR,
            ],
            compiler_params=pltpu.CompilerParams(
                collective_id=0, has_side_effects=True, vmem_limit_bytes=24 * 2**20
            ),
            cost_estimate=pl.CostEstimate(
                flops=2 * 30 * nb**3, bytes_accessed=4 * 10 * nb * nb, transcendentals=0
            ),
            name="chase",
        )(offsets, plan, eigvecs, refl_v, refl_t)
        return lax.dynamic_slice(y, (nb - offsets[0], 0), (own, width))

    return jax.shard_map(
        on_device,
        mesh=mesh,
        in_specs=(P("row", "col"), P(), P(), P("col", None, None), P("col", None, None)),
        out_specs=P("row", "col"),
        check_vma=False,
    )
```

```python
import functools

import jax
import jax.numpy as jnp
from jax import lax
from jax.experimental import pallas as pl
from jax.experimental.pallas import tpu as pltpu
from jax.sharding import PartitionSpec as P

MESH = pl.DeviceIdType.MESH
F32 = jnp.float32
BF16 = jnp.bfloat16


def split(a):
    hi = a.astype(BF16)
    return hi, (a - hi.astype(F32)).astype(BF16)


def mm(a, b, rhs_t=False):
    dims = (((1,), (1 if rhs_t else 0,)), ((), ()))
    ah, al = split(a)
    bh, bl = split(b)
    dot = functools.partial(
        lax.dot_general, dimension_numbers=dims, preferred_element_type=F32
    )
    return dot(ah, bl) + dot(al, bh) + dot(ah, bh)


def both(pair):
    return jnp.concatenate([pair[0], pair[1]], axis=1)


def classes(cols):
    if cols == 32:
        start_z = (0.0, 0.9, 1.9, 2.8, 5.8, 6.7, 7.6, 8.4)
        start_y = (0.4, 2.2, 4.7, 3.3)
        start = {4 * z + y: start_z[z] + start_y[y] for z in range(8) for y in range(4)}
        served = {
            (7, 0): (1, 0), (5, 1): (4, 0), (6, 1): (3, 1), (7, 1): (0, 1),
            (4, 2): (3, 2), (5, 2): (4, 1), (6, 2): (1, 2), (7, 2): (0, 2),
            (4, 3): (3, 3), (5, 3): (5, 0), (6, 3): (6, 0), (7, 3): (0, 3),
        }
        partner = {4 * a + b: 4 * d + e for (a, b), (d, e) in served.items()}
    else:
        start = {k: k for k in range(cols)}
        partner = {k: k - cols // 2 for k in range((cols + 1) // 2, cols)}
    order = sorted(start, key=lambda k: start[k])
    return [k for k in order if k not in partner], partner


def kernel(
    rows, cols, off_hbm, plan_hbm, e_ref, v_ref, t_ref, y_ref,
    off_ref, plan_ref, xin, low, up, mine, g1, stage, g2, g3, ebuf, p1buf, fbuf, abuf, hbuf, bbuf, pbuf, sbuf, cbuf, dbuf,
    lsem, hsem, s1, s2, s3, psem, asem, bsend, brecv, dsem, qsem, rowsem,
):
    nb = t_ref.shape[1]
    part = nb // rows
    own = e_ref.shape[0]
    r = lax.axis_index("row")
    c = lax.axis_index("col")
    core, pair, x = r % 2, (r // 2) % 2, r // 4
    groups = rows // 4
    early, partner = classes(cols)
    blocks = 2 * rows - 2

    is_late = functools.reduce(jnp.logical_or, [c == k for k in partner])
    serves = functools.reduce(jnp.logical_or, [c == k for k in partner.values()])
    other = sum(
        jnp.where(c == a, b, 0) + jnp.where(c == b, a, 0) for a, b in partner.items()
    )
    is_early = jnp.logical_not(is_late)

    def row_at(k):
        return lax.rem(r + k, rows)

    def remote(src, dst, send, recv, to_row, to_col):
        return pltpu.make_async_remote_copy(
            src_ref=src, dst_ref=dst, send_sem=send, recv_sem=recv,
            device_id=(to_row, to_col), device_id_type=MESH,
        )

    def signal(sem, to_row, to_col):
        pl.semaphore_signal(sem, 1, device_id=(to_row, to_col), device_id_type=MESH)

    def await_bytes(ref, sem):
        pltpu.make_async_copy(ref, ref, sem).wait()

    at = pl.multiple_of(r * part, part)
    end = jnp.minimum(nb + at + part - 1, 2 * nb - 2)
    get_low = pltpu.make_async_copy(v_ref.at[pl.ds(at, part), 0], low, lsem.at[0])
    get_up = pltpu.make_async_copy(
        v_ref.at[pl.ds(nb + at, part - 1), 0], up.at[pl.ds(0, part - 1)], lsem.at[1]
    )
    get_end = pltpu.make_async_copy(
        v_ref.at[pl.ds(end, 1), 0], up.at[pl.ds(part - 1, 1)], lsem.at[5]
    )
    get_t = pltpu.make_async_copy(
        t_ref.at[0, pl.ds(at, part)], mine.at[pl.ds(part, part)], lsem.at[6]
    )
    mine_parts = (get_low, get_up, get_end, get_t)
    get_e = pltpu.make_async_copy(e_ref, xin.at[pl.ds(nb, own)], lsem.at[2])
    get_plan = pltpu.make_async_copy(plan_hbm, plan_ref, lsem.at[3])
    get_off = pltpu.make_async_copy(off_hbm, off_ref, lsem.at[4])
    for copy in mine_parts + (get_e, get_plan, get_off):
        copy.start()

    barrier = pltpu.get_barrier_semaphore()

    @pl.when(is_early)
    def _():
        for k in list(partner) + early[::-1]:
            @pl.when(c != k)
            def _(k=k):
                signal(barrier, r, k)
        for k in range(1, rows):
            signal(barrier, row_at(k), c)

        @pl.when(serves)
        def _():
            for k in range(1, rows):
                signal(barrier, row_at(k), other)

    xin[0:nb] = jnp.zeros((nb, nb), F32)
    for copy in mine_parts:
        copy.wait()
    row_ids = lax.broadcasted_iota(jnp.int32, (part, nb), 0) + at
    col_ids = lax.broadcasted_iota(jnp.int32, (part, nb), 1)
    mine[0:part] = jnp.where(row_ids >= col_ids, low[...], up[...])

    pl.semaphore_wait(barrier, len(early) + rows - 1 - is_early.astype(jnp.int32))

    for k in early:
        @pl.when(c != k)
        def _(k=k):
            remote(mine, g1.at[c], s1.at[0], s1.at[1], r, k).start()

    head = remote(
        e_ref, xin.at[pl.ds(nb + own, own)], hsem.at[0], hsem.at[1], row_at(rows - 1), c
    )

    @pl.when(is_early)
    def _():
        head.start()
        g1[c] = mine[...]
        await_bytes(g1.at[pl.ds(0, cols - 1)], s1.at[1])

    @pl.when(is_late)
    def _():
        for k in range(1, rows):
            signal(rowsem, row_at(k), other)
        await_bytes(g1, s1.at[1])
        head.start()

    get_plan.wait()
    get_off.wait()

    order = sorted(range(1, rows), key=lambda k: -min(k, rows - k)) + [0]

    def pick(to, j):
        return g1[plan_ref[0, jnp.clip(2 * to - 1 + j, 0, blocks - 1)]]

    for k in order:
        to = row_at(k)
        dst = stage.at[k] if k else g2.at[r]
        dst[0 : 2 * part] = pick(to, 0)
        dst[2 * part : 4 * part] = pick(to, 1)
        if k:
            remote(stage.at[k], g2.at[r], s2.at[0], s2.at[1], to, c).start()

    relay = remote(g1, g1, qsem.at[0], s1.at[1], r, other)

    @pl.when(serves)
    def _():
        pl.semaphore_wait(rowsem, rows - 1)
        relay.start()

    get_e.wait()
    head.wait_recv()
    off = off_ref[0]
    s0 = xin[pl.ds(off, nb)]

    ri = lax.broadcasted_iota(jnp.int32, (nb, nb), 0)
    ci = lax.broadcasted_iota(jnp.int32, (nb, nb), 1)
    eye = (ri == ci).astype(F32)

    def block_map(j, packed, factor):
        number = 2 * r - 1 + j
        live = ((number >= 0) & (number < blocks)).astype(F32)
        fresh = xin[pl.ds(off + nb * (1 + j), nb)]
        packed = packed.reshape(nb, nb)
        factor = factor.reshape(nb, nb) * live
        lower = jnp.where(ri >= ci, packed, 0.0)
        upper = jnp.where(ri >= ci, 0.0, packed)
        vectors = jnp.concatenate([lower, upper], axis=0)
        tv = mm(factor, vectors, rhs_t=True)
        m, n = tv[:, :nb], tv[:, nb:]
        z = mm(n, fresh)
        w = mm(vectors if j < 2 else lower, jnp.concatenate([m, z], axis=1))
        if j == 2:
            return eye - w[:, :nb], -w[:, nb:]
        return eye - w[:nb, :nb], -w[:nb, nb:], -w[nb:, :nb], fresh - w[nb:, nb:]

    await_bytes(g2.at[pl.ds(0, rows - 1)], s2.at[1])

    third = remote(
        g2.at[:, pl.ds(0, 2 * part)], g3, s3.at[0], s3.at[1], row_at(rows - 1), c
    )
    third.start()
    c0, d0, a0, b0 = block_map(0, g2[:, 0:part], g2[:, part : 2 * part])
    c1, d1, a1, b1 = block_map(1, g2[:, 2 * part : 3 * part], g2[:, 3 * part : 4 * part])
    w = mm(jnp.concatenate([a1, c1], axis=0), jnp.concatenate([a0, b0], axis=1))
    ebuf[0] = w[:nb, :nb]
    ebuf[1] = w[:nb, nb:] + b1

    to_core1 = remote(ebuf, p1buf, psem.at[0], psem.at[1], r ^ 1, c)
    to_pair = remote(fbuf, abuf, asem.at[0], asem.at[1], r ^ 2, c)
    prefix = remote(abuf, pbuf, psem.at[0], psem.at[1], r ^ 1, c)
    state = remote(sbuf, sbuf, dsem.at[0], dsem.at[1], r ^ 1, c)
    core0, core1 = core == 0, core == 1

    @pl.when(core0)
    def _():
        to_core1.start()

    cbuf[0:nb] = c0
    dbuf[0:nb] = d0
    cbuf[nb : 2 * nb] = w[nb:, :nb]
    dbuf[nb : 2 * nb] = w[nb:, nb:] + d1

    @pl.when(core1)
    def _():
        to_core1.wait_recv()
        w = mm(ebuf[0], both(p1buf))
        fbuf[0] = w[:, :nb]
        fbuf[1] = w[:, nb:] + ebuf[1]
        to_pair.start()

    third.wait_recv()
    c2, d2 = block_map(2, g3[:, 0:part], g3[:, part : 2 * part])
    w = mm(c2, both(ebuf))
    cbuf[2 * nb : 3 * nb] = w[:, :nb]
    dbuf[2 * nb : 3 * nb] = w[:, nb:] + d2

    def along_x(step, half):
        return remote(
            hbuf.at[half], bbuf.at[x, half], bsend.at[step, half], brecv.at[x, half],
            lax.rem(r + 4 * step, rows), c,
        )

    @pl.when(core1)
    def _():
        to_pair.wait_recv()
        first = pair == 0

        @pl.when(pair == 1)
        def _():
            prefix.start()

        late_g = jnp.where(first, abuf[0], fbuf[0])
        late_b = jnp.where(first, abuf[1], fbuf[1])
        early_pair = jnp.where(first, both(fbuf), both(abuf))
        w = mm(late_g, early_pair)
        hbuf[0] = w[:, :nb]
        hbuf[1] = w[:, nb:] + late_b
        for step in range(1, groups):
            @pl.when(x + step < groups)
            def _(step=step):
                along_x(step, 1).start()

                @pl.when(x > 0)
                def _():
                    along_x(step, 0).start()

        @pl.when(pair == 0)
        def _():
            pbuf[...] = p1buf[...]

        @pl.when(pair == 1)
        def _():
            w = mm(p1buf[0], both(abuf))
            pbuf[0] = w[:, :nb]
            pbuf[1] = w[:, nb:] + p1buf[1]

    @pl.when(core0 & (pair == 1))
    def _():
        prefix.wait_recv()

    @pl.when(core1 | (pair == 1))
    def _():
        w = mm(cbuf[...], both(pbuf))
        cbuf[...] = w[:, :nb]
        dbuf[...] = w[:, nb:] + dbuf[...]

    @pl.when(x == 0)
    def _():
        sbuf[...] = s0

    @pl.when((x > 0) & core1)
    def _():
        for source in range(groups - 1):
            @pl.when(x > source)
            def _(source=source):
                await_bytes(bbuf.at[source, 1], brecv.at[source, 1])
                if source:
                    await_bytes(bbuf.at[source, 0], brecv.at[source, 0])
                    sbuf[...] = mm(bbuf[source, 0], sbuf[...]) + bbuf[source, 1]
                else:
                    sbuf[...] = bbuf[source, 1]
        state.start()

    @pl.when((x > 0) & core0)
    def _():
        state.wait_recv()

    y_ref[...] = mm(cbuf[...], sbuf[...]) + dbuf[...]

    sent = g1.at[pl.ds(0, len(early) - 1)]
    await_bytes(sent, s1.at[0])
    head.wait_send()
    await_bytes(g2.at[pl.ds(0, rows - 1)], s2.at[0])
    third.wait_send()

    @pl.when(is_late)
    def _():
        await_bytes(g1.at[0], s1.at[0])

    @pl.when(serves)
    def _():
        relay.wait_send()

    @pl.when(core0)
    def _():
        to_core1.wait_send()

    @pl.when(core1)
    def _():
        to_pair.wait_send()

        @pl.when(pair == 1)
        def _():
            prefix.wait_send()

        @pl.when(x > 0)
        def _():
            state.wait_send()

        for step in range(1, groups):
            @pl.when(x + step < groups)
            def _(step=step):
                along_x(step, 1).wait_send()

                @pl.when(x > 0)
                def _():
                    along_x(step, 0).wait_send()


def solution(mesh):
    rows, cols = mesh.shape["row"], mesh.shape["col"]

    def on_device(eigvecs, offsets, plan, refl_v, refl_t):
        own, width = eigvecs.shape
        nb = refl_t.shape[1]
        part = nb // rows
        dma = pltpu.SemaphoreType.DMA
        square = (nb, nb)
        y = pl.pallas_call(
            functools.partial(kernel, rows, cols),
            out_shape=jax.ShapeDtypeStruct((3 * nb, width), F32),
            in_specs=[
                pl.BlockSpec(memory_space=pl.ANY),
                pl.BlockSpec(memory_space=pl.ANY),
                pl.BlockSpec(memory_space=pl.ANY),
                pl.BlockSpec(memory_space=pl.ANY),
                pl.BlockSpec(memory_space=pl.ANY),
            ],
            out_specs=pl.BlockSpec(memory_space=pltpu.VMEM),
            scratch_shapes=[
                pltpu.SMEM(offsets.shape, jnp.int32),
                pltpu.SMEM(plan.shape, jnp.int32),
                pltpu.VMEM((nb + 2 * own, width), F32),
                pltpu.VMEM((part, nb), F32),
                pltpu.VMEM((part, nb), F32),
                pltpu.VMEM((2 * part, nb), F32),
                pltpu.VMEM((cols, 2 * part, nb), F32),
                pltpu.VMEM((rows, 4 * part, nb), F32),
                pltpu.VMEM((rows, 4 * part, nb), F32),
                pltpu.VMEM((rows, 2 * part, nb), F32),
                pltpu.VMEM((2,) + square, F32),
                pltpu.VMEM((2,) + square, F32),
                pltpu.VMEM((2,) + square, F32),
                pltpu.VMEM((2,) + square, F32),
                pltpu.VMEM((2,) + square, F32),
                pltpu.VMEM((rows // 4, 2) + square, F32),
                pltpu.VMEM((2,) + square, F32),
                pltpu.VMEM(square, F32),
                pltpu.VMEM((3 * nb, nb), F32),
                pltpu.VMEM((3 * nb, width), F32),
                dma((7,)), dma((2,)), dma((2,)), dma((2,)), dma((2,)), dma((2,)), dma((2,)),
                dma((rows // 4, 2)), dma((rows // 4, 2)), dma((2,)), dma((1,)),
                pltpu.SemaphoreType.REGULAR,
            ],
            compiler_params=pltpu.CompilerParams(
                collective_id=0, has_side_effects=True, vmem_limit_bytes=60 * 2**20
            ),
            cost_estimate=pl.CostEstimate(
                flops=2 * 30 * nb**3, bytes_accessed=4 * 10 * nb * nb, transcendentals=0
            ),
            name="chase",
        )(offsets, plan, eigvecs, refl_v.transpose(1, 0, 2), refl_t)
        return lax.dynamic_slice(y, (nb - offsets[0], 0), (own, width))

    return jax.shard_map(
        on_device,
        mesh=mesh,
        in_specs=(P("row", "col"), P(), P(), P("col", None, None), P("col", None, None)),
        out_specs=P("row", "col"),
        check_vma=False,
    )
```

```python
import functools

import jax
import jax.numpy as jnp
from jax import lax
from jax.experimental import pallas as pl
from jax.experimental.pallas import tpu as pltpu
from jax.sharding import PartitionSpec as P

MESH = pl.DeviceIdType.MESH
F32 = jnp.float32
BF16 = jnp.bfloat16


def split(a):
    hi = a.astype(BF16)
    return hi, (a - hi.astype(F32)).astype(BF16)


def mm(a, b, rhs_t=False):
    dims = (((1,), (1 if rhs_t else 0,)), ((), ()))
    ah, al = split(a)
    bh, bl = split(b)
    dot = functools.partial(
        lax.dot_general, dimension_numbers=dims, preferred_element_type=F32
    )
    return dot(ah, bl) + dot(al, bh) + dot(ah, bh)


def both(pair):
    return jnp.concatenate([pair[0], pair[1]], axis=1)


def classes(cols):
    if cols == 32:
        start_z = (0.0, 0.9, 1.9, 2.8, 5.8, 6.7, 7.6, 8.4)
        start_y = (0.4, 2.2, 4.7, 3.3)
        start = {4 * z + y: start_z[z] + start_y[y] for z in range(8) for y in range(4)}
        served = {
            (7, 0): (1, 0), (5, 1): (4, 0), (6, 1): (3, 1), (7, 1): (0, 1),
            (4, 2): (3, 2), (5, 2): (4, 1), (6, 2): (1, 2), (7, 2): (0, 2),
            (4, 3): (3, 3), (5, 3): (5, 0), (6, 3): (6, 0), (7, 3): (0, 3),
        }
        partner = {4 * a + b: 4 * d + e for (a, b), (d, e) in served.items()}
    else:
        start = {k: k for k in range(cols)}
        partner = {k: k - cols // 2 for k in range((cols + 1) // 2, cols)}
    order = sorted(start, key=lambda k: start[k])
    early = [k for k in order if k not in partner]
    return early, [k for k in order if k in partner], partner


def kernel(
    rows, cols, off_hbm, plan_hbm, e_ref, v_ref, t_ref, y_ref,
    off_ref, plan_ref, xin, low, up, mine, g1, stage, g2, g3, ebuf, p1buf, fbuf, abuf, hbuf, bbuf, pbuf, sbuf, cbuf, dbuf,
    lsem, hsem, s1, s2, s3, psem, asem, bsend, brecv, dsem, rowsem, gosem,
):
    nb = t_ref.shape[1]
    part = nb // rows
    own = e_ref.shape[0]
    r = lax.axis_index("row")
    c = lax.axis_index("col")
    core, pair, x = r % 2, (r // 2) % 2, r // 4
    groups = rows // 4
    early, late, partner = classes(cols)
    blocks = 2 * rows - 2

    is_late = functools.reduce(jnp.logical_or, [c == k for k in partner])
    serves = functools.reduce(jnp.logical_or, [c == k for k in partner.values()])
    other = sum(
        jnp.where(c == a, b, 0) + jnp.where(c == b, a, 0) for a, b in partner.items()
    )
    is_early = jnp.logical_not(is_late)

    def row_at(k):
        return lax.rem(r + k, rows)

    def remote(src, dst, send, recv, to_row, to_col):
        return pltpu.make_async_remote_copy(
            src_ref=src, dst_ref=dst, send_sem=send, recv_sem=recv,
            device_id=(to_row, to_col), device_id_type=MESH,
        )

    def signal(sem, to_row, to_col):
        pl.semaphore_signal(sem, 1, device_id=(to_row, to_col), device_id_type=MESH)

    def await_bytes(ref, sem):
        pltpu.make_async_copy(ref, ref, sem).wait()

    at = pl.multiple_of(r * part, part)
    end = jnp.minimum(nb + at + part - 1, 2 * nb - 2)
    get_low = pltpu.make_async_copy(v_ref.at[pl.ds(at, part), 0], low, lsem.at[0])
    get_up = pltpu.make_async_copy(
        v_ref.at[pl.ds(nb + at, part - 1), 0], up.at[pl.ds(0, part - 1)], lsem.at[1]
    )
    get_end = pltpu.make_async_copy(
        v_ref.at[pl.ds(end, 1), 0], up.at[pl.ds(part - 1, 1)], lsem.at[5]
    )
    get_t = pltpu.make_async_copy(
        t_ref.at[0, pl.ds(at, part)], mine.at[pl.ds(part, part)], lsem.at[6]
    )
    mine_parts = (get_low, get_up, get_end, get_t)
    get_e = pltpu.make_async_copy(e_ref, xin.at[pl.ds(nb, own)], lsem.at[2])
    get_plan = pltpu.make_async_copy(plan_hbm, plan_ref, lsem.at[3])
    get_off = pltpu.make_async_copy(off_hbm, off_ref, lsem.at[4])
    for copy in mine_parts + (get_e, get_plan, get_off):
        copy.start()

    barrier = pltpu.get_barrier_semaphore()

    @pl.when(is_early)
    def _():
        for k in list(partner) + early[::-1]:
            @pl.when(c != k)
            def _(k=k):
                signal(barrier, r, k)
        for k in range(1, rows):
            signal(barrier, row_at(k), c)

        @pl.when(serves)
        def _():
            for k in range(1, rows):
                signal(barrier, row_at(k), other)

    xin[0:nb] = jnp.zeros((nb, nb), F32)
    for copy in mine_parts:
        copy.wait()
    row_ids = lax.broadcasted_iota(jnp.int32, (part, nb), 0) + at
    col_ids = lax.broadcasted_iota(jnp.int32, (part, nb), 1)
    mine[0:part] = jnp.where(row_ids >= col_ids, low[...], up[...])

    pl.semaphore_wait(barrier, len(early) + rows - 1 - is_early.astype(jnp.int32))

    def share(to, own_class):
        for k in to:
            @pl.when((c != k) & own_class)
            def _(k=k):
                remote(mine, g1.at[c], s1.at[0], s1.at[1], r, k).start()

    share(early, True)
    head = remote(
        e_ref, xin.at[pl.ds(nb + own, own)], hsem.at[0], hsem.at[1], row_at(rows - 1), c
    )
    got1 = g1.at[pl.ds(0, cols - 1)]
    g1[c] = mine[...]

    @pl.when(is_early)
    def _():
        head.start()
        await_bytes(got1, s1.at[1])

        @pl.when(serves)
        def _():
            pl.semaphore_wait(rowsem, rows - 1)
            signal(gosem, r, other)

    @pl.when(is_late)
    def _():
        for k in range(1, rows):
            signal(rowsem, row_at(k), other)
        pl.semaphore_wait(gosem, 1)
        share(late, True)
        head.start()
        await_bytes(got1, s1.at[1])

    get_plan.wait()
    get_off.wait()

    order = sorted(range(1, rows), key=lambda k: -min(k, rows - k)) + [0]
    for k in order:
        dst = stage.at[k] if k else g2.at[r]
        for j in range(2):
            block = jnp.clip(2 * row_at(k) - 1 + j, 0, blocks - 1)
            dst[2 * part * j : 2 * part * (j + 1)] = g1[plan_ref[0, block]]
    for k in order[:-1]:
        remote(stage.at[k], g2.at[r], s2.at[0], s2.at[1], row_at(k), c).start()
    share(late, is_early)

    get_e.wait()
    head.wait_recv()
    off = off_ref[0]
    s0 = xin[pl.ds(off, nb)]

    ri = lax.broadcasted_iota(jnp.int32, (nb, nb), 0)
    ci = lax.broadcasted_iota(jnp.int32, (nb, nb), 1)
    eye = (ri == ci).astype(F32)

    def block_map(j, packed, factor):
        number = 2 * r - 1 + j
        live = ((number >= 0) & (number < blocks)).astype(F32)
        fresh = xin[pl.ds(off + nb * (1 + j), nb)]
        packed = packed.reshape(nb, nb)
        factor = factor.reshape(nb, nb) * live
        lower = jnp.where(ri >= ci, packed, 0.0)
        upper = jnp.where(ri >= ci, 0.0, packed)
        vectors = jnp.concatenate([lower, upper], axis=0)
        tv = mm(factor, vectors, rhs_t=True)
        m, n = tv[:, :nb], tv[:, nb:]
        z = mm(n, fresh)
        w = mm(vectors if j < 2 else lower, jnp.concatenate([m, z], axis=1))
        if j == 2:
            return eye - w[:, :nb], -w[:, nb:]
        return eye - w[:nb, :nb], -w[:nb, nb:], -w[nb:, :nb], fresh - w[nb:, nb:]

    await_bytes(g2.at[pl.ds(0, rows - 1)], s2.at[1])

    third = remote(
        g2.at[:, pl.ds(0, 2 * part)], g3, s3.at[0], s3.at[1], row_at(rows - 1), c
    )
    third.start()
    c0, d0, a0, b0 = block_map(0, g2[:, 0:part], g2[:, part : 2 * part])
    c1, d1, a1, b1 = block_map(1, g2[:, 2 * part : 3 * part], g2[:, 3 * part : 4 * part])
    w = mm(jnp.concatenate([a1, c1], axis=0), jnp.concatenate([a0, b0], axis=1))
    ebuf[0] = w[:nb, :nb]
    ebuf[1] = w[:nb, nb:] + b1

    to_core1 = remote(ebuf, p1buf, psem.at[0], psem.at[1], r ^ 1, c)
    to_pair = remote(fbuf, abuf, asem.at[0], asem.at[1], r ^ 2, c)
    prefix = remote(abuf, pbuf, psem.at[0], psem.at[1], r ^ 1, c)
    state = remote(sbuf, sbuf, dsem.at[0], dsem.at[1], r ^ 1, c)
    core0, core1 = core == 0, core == 1

    @pl.when(core0)
    def _():
        to_core1.start()

    cbuf[0:nb] = c0
    dbuf[0:nb] = d0
    cbuf[nb : 2 * nb] = w[nb:, :nb]
    dbuf[nb : 2 * nb] = w[nb:, nb:] + d1

    @pl.when(core1)
    def _():
        to_core1.wait_recv()
        w = mm(ebuf[0], both(p1buf))
        fbuf[0] = w[:, :nb]
        fbuf[1] = w[:, nb:] + ebuf[1]
        to_pair.start()

    third.wait_recv()
    c2, d2 = block_map(2, g3[:, 0:part], g3[:, part : 2 * part])
    w = mm(c2, both(ebuf))
    cbuf[2 * nb : 3 * nb] = w[:, :nb]
    dbuf[2 * nb : 3 * nb] = w[:, nb:] + d2

    def along_x(step, half):
        return remote(
            hbuf.at[half], bbuf.at[x, half], bsend.at[step, half], brecv.at[x, half],
            lax.rem(r + 4 * step, rows), c,
        )

    @pl.when(core1)
    def _():
        to_pair.wait_recv()
        first = pair == 0

        @pl.when(pair == 1)
        def _():
            prefix.start()

        late_g = jnp.where(first, abuf[0], fbuf[0])
        late_b = jnp.where(first, abuf[1], fbuf[1])
        early_pair = jnp.where(first, both(fbuf), both(abuf))
        w = mm(late_g, early_pair)
        hbuf[0] = w[:, :nb]
        hbuf[1] = w[:, nb:] + late_b
        for step in range(1, groups):
            @pl.when(x + step < groups)
            def _(step=step):
                along_x(step, 1).start()

                @pl.when(x > 0)
                def _():
                    along_x(step, 0).start()

        @pl.when(pair == 0)
        def _():
            pbuf[...] = p1buf[...]

        @pl.when(pair == 1)
        def _():
            w = mm(p1buf[0], both(abuf))
            pbuf[0] = w[:, :nb]
            pbuf[1] = w[:, nb:] + p1buf[1]

    @pl.when(core0 & (pair == 1))
    def _():
        prefix.wait_recv()

    @pl.when(core1 | (pair == 1))
    def _():
        w = mm(cbuf[...], both(pbuf))
        cbuf[...] = w[:, :nb]
        dbuf[...] = w[:, nb:] + dbuf[...]

    @pl.when(x == 0)
    def _():
        sbuf[...] = s0

    @pl.when((x > 0) & core1)
    def _():
        for source in range(groups - 1):
            @pl.when(x > source)
            def _(source=source):
                await_bytes(bbuf.at[source, 1], brecv.at[source, 1])
                if source:
                    await_bytes(bbuf.at[source, 0], brecv.at[source, 0])
                    sbuf[...] = mm(bbuf[source, 0], sbuf[...]) + bbuf[source, 1]
                else:
                    sbuf[...] = bbuf[source, 1]
        state.start()

    @pl.when((x > 0) & core0)
    def _():
        state.wait_recv()

    y_ref[...] = mm(cbuf[...], sbuf[...]) + dbuf[...]

    await_bytes(got1, s1.at[0])
    head.wait_send()
    await_bytes(g2.at[pl.ds(0, rows - 1)], s2.at[0])
    third.wait_send()

    @pl.when(core0)
    def _():
        to_core1.wait_send()

    @pl.when(core1)
    def _():
        to_pair.wait_send()

        @pl.when(pair == 1)
        def _():
            prefix.wait_send()

        @pl.when(x > 0)
        def _():
            state.wait_send()

        for step in range(1, groups):
            @pl.when(x + step < groups)
            def _(step=step):
                along_x(step, 1).wait_send()

                @pl.when(x > 0)
                def _():
                    along_x(step, 0).wait_send()


def solution(mesh):
    rows, cols = mesh.shape["row"], mesh.shape["col"]

    def on_device(eigvecs, offsets, plan, refl_v, refl_t):
        own, width = eigvecs.shape
        nb = refl_t.shape[1]
        part = nb // rows
        dma = pltpu.SemaphoreType.DMA
        square = (nb, nb)
        y = pl.pallas_call(
            functools.partial(kernel, rows, cols),
            out_shape=pltpu.VMEM((3 * nb, width), F32),
            in_specs=[
                pl.BlockSpec(memory_space=pl.ANY),
                pl.BlockSpec(memory_space=pl.ANY),
                pl.BlockSpec(memory_space=pl.ANY),
                pl.BlockSpec(memory_space=pl.ANY),
                pl.BlockSpec(memory_space=pl.ANY),
            ],
            out_specs=pl.BlockSpec(memory_space=pltpu.VMEM),
            scratch_shapes=[
                pltpu.SMEM(offsets.shape, jnp.int32),
                pltpu.SMEM(plan.shape, jnp.int32),
                pltpu.VMEM((nb + 2 * own, width), F32),
                pltpu.VMEM((part, nb), F32),
                pltpu.VMEM((part, nb), F32),
                pltpu.VMEM((2 * part, nb), F32),
                pltpu.VMEM((cols, 2 * part, nb), F32),
                pltpu.VMEM((rows, 4 * part, nb), F32),
                pltpu.VMEM((rows, 4 * part, nb), F32),
                pltpu.VMEM((rows, 2 * part, nb), F32),
                pltpu.VMEM((2,) + square, F32),
                pltpu.VMEM((2,) + square, F32),
                pltpu.VMEM((2,) + square, F32),
                pltpu.VMEM((2,) + square, F32),
                pltpu.VMEM((2,) + square, F32),
                pltpu.VMEM((rows // 4, 2) + square, F32),
                pltpu.VMEM((2,) + square, F32),
                pltpu.VMEM(square, F32),
                pltpu.VMEM((3 * nb, nb), F32),
                pltpu.VMEM((3 * nb, width), F32),
                dma((7,)), dma((2,)), dma((2,)), dma((2,)), dma((2,)), dma((2,)), dma((2,)),
                dma((rows // 4, 2)), dma((rows // 4, 2)), dma((2,)),
                pltpu.SemaphoreType.REGULAR, pltpu.SemaphoreType.REGULAR,
            ],
            compiler_params=pltpu.CompilerParams(
                collective_id=0, has_side_effects=True, vmem_limit_bytes=60 * 2**20
            ),
            cost_estimate=pl.CostEstimate(
                flops=2 * 30 * nb**3, bytes_accessed=4 * 10 * nb * nb, transcendentals=0
            ),
            name="chase",
        )(offsets, plan, eigvecs, refl_v.transpose(1, 0, 2), refl_t)
        return lax.dynamic_slice(y, (nb - offsets[0], 0), (own, width))

    return jax.shard_map(
        on_device,
        mesh=mesh,
        in_specs=(P("row", "col"), P(), P(), P("col", None, None), P("col", None, None)),
        out_specs=P("row", "col"),
        check_vma=False,
    )
```

```python
import functools

import jax
import jax.numpy as jnp
from jax import lax
from jax.experimental import pallas as pl
from jax.experimental.pallas import tpu as pltpu
from jax.sharding import PartitionSpec as P

MESH = pl.DeviceIdType.MESH
F32 = jnp.float32
BF16 = jnp.bfloat16


def split(a):
    hi = a.astype(BF16)
    return hi, (a - hi.astype(F32)).astype(BF16)


def mm(a, b, rhs_t=False):
    dims = (((1,), (1 if rhs_t else 0,)), ((), ()))
    ah, al = split(a)
    bh, bl = split(b)
    dot = functools.partial(
        lax.dot_general, dimension_numbers=dims, preferred_element_type=F32
    )
    return dot(ah, bl) + dot(al, bh) + dot(ah, bh)


def both(pair):
    return jnp.concatenate([pair[0], pair[1]], axis=1)


def classes(cols):
    if cols == 32:
        start_z = (0.0, 0.9, 1.9, 2.8, 5.8, 6.7, 7.6, 8.4)
        start_y = (0.4, 2.2, 4.7, 3.3)
        start = {4 * z + y: start_z[z] + start_y[y] for z in range(8) for y in range(4)}
        served = {(7, 0): (6, 0), (5, 1): (4, 1), (6, 1): (3, 1), (7, 1): (0, 1)}
        for y in (2, 3):
            served.update({(4 + k, y): (3 - k, y) for k in range(4)})
        partner = {4 * a + b: 4 * d + e for (a, b), (d, e) in served.items()}
    else:
        start = {k: k for k in range(cols)}
        partner = {k: k - cols // 2 for k in range((cols + 1) // 2, cols)}
    order = sorted(start, key=lambda k: start[k])
    early = [k for k in order if k not in partner]
    return early, [k for k in order if k in partner], partner


def kernel(
    rows, cols, off_hbm, plan_hbm, e_ref, v_ref, t_ref, y_ref,
    off_ref, plan_ref, xin, low, up, mine, g1, stage, g2, g3, ebuf, p1buf, fbuf, abuf, hbuf, bbuf, pbuf, sbuf, cbuf, dbuf,
    lsem, msem, hsem, s1, s2, s3, psem, asem, bsend, brecv, dsem, rowsem, colsem, gosem,
):
    nb = t_ref.shape[1]
    part = nb // rows
    own = e_ref.shape[0]
    r = lax.axis_index("row")
    c = lax.axis_index("col")
    core, pair, x = r % 2, (r // 2) % 2, r // 4
    groups = rows // 4
    early, late, partner = classes(cols)
    blocks = 2 * rows - 2

    is_late = functools.reduce(jnp.logical_or, [c == k for k in partner])
    serves = functools.reduce(jnp.logical_or, [c == k for k in partner.values()])
    other = sum(
        jnp.where(c == a, b, 0) + jnp.where(c == b, a, 0) for a, b in partner.items()
    )
    is_early = jnp.logical_not(is_late)

    def row_at(k):
        return lax.rem(r + k, rows)

    swaps = cols % 8 == 0

    def across(k):
        return (lax.rem(c - k + 4 * cols, 4) == 2).astype(jnp.int32) if swaps else 0

    def row_for(k):
        return r ^ (2 * across(k))

    def remote(src, dst, send, recv, to_row, to_col):
        return pltpu.make_async_remote_copy(
            src_ref=src, dst_ref=dst, send_sem=send, recv_sem=recv,
            device_id=(to_row, to_col), device_id_type=MESH,
        )

    def signal(sem, to_row, to_col):
        pl.semaphore_signal(sem, 1, device_id=(to_row, to_col), device_id_type=MESH)

    def await_bytes(ref, sem):
        pltpu.make_async_copy(ref, ref, sem).wait()

    mine_parts = []
    for i in range(1 + swaps):
        at = pl.multiple_of((r ^ (2 * i)) * part, part)
        end = jnp.minimum(nb + at + part - 1, 2 * nb - 2)
        mine_parts += [
            pltpu.make_async_copy(v_ref.at[pl.ds(at, part), 0], low.at[i], msem.at[i, 0]),
            pltpu.make_async_copy(
                v_ref.at[pl.ds(nb + at, part - 1), 0],
                up.at[i, pl.ds(0, part - 1)],
                msem.at[i, 1],
            ),
            pltpu.make_async_copy(
                v_ref.at[pl.ds(end, 1), 0], up.at[i, pl.ds(part - 1, 1)], msem.at[i, 2]
            ),
            pltpu.make_async_copy(
                t_ref.at[0, pl.ds(at, part)], mine.at[i, pl.ds(part, part)], msem.at[i, 3]
            ),
        ]
    get_e = pltpu.make_async_copy(e_ref, xin.at[pl.ds(nb, own)], lsem.at[0])
    get_plan = pltpu.make_async_copy(plan_hbm, plan_ref, lsem.at[1])
    get_off = pltpu.make_async_copy(off_hbm, off_ref, lsem.at[2])
    for copy in mine_parts + [get_e, get_plan, get_off]:
        copy.start()

    barrier = pltpu.get_barrier_semaphore()

    @pl.when(is_early)
    def _():
        for k in late[::-1] + early[::-1]:
            @pl.when(c != k)
            def _(k=k):
                signal(barrier, row_for(k), k)
        for k in range(1, rows):
            signal(barrier, row_at(k), c)

        @pl.when(serves)
        def _():
            for k in range(1, rows):
                signal(barrier, row_at(k), other)

    @pl.when(is_late)
    def _():
        pl.semaphore_wait(barrier, len(early) + rows - 1)
        for k in early:
            signal(colsem, row_for(k), k)
        for k in range(1, rows):
            signal(rowsem, row_at(k), other)

    xin[0:nb] = jnp.zeros((nb, nb), F32)
    for copy in mine_parts:
        copy.wait()
    for i in range(1 + swaps):
        at = (r ^ (2 * i)) * part
        row_ids = lax.broadcasted_iota(jnp.int32, (part, nb), 0) + at
        col_ids = lax.broadcasted_iota(jnp.int32, (part, nb), 1)
        mine[i, 0:part] = jnp.where(row_ids >= col_ids, low[i], up[i])

    @pl.when(is_early)
    def _():
        pl.semaphore_wait(barrier, len(early) - 1 + rows - 1)

    def share(to):
        for k in to:
            @pl.when(c != k)
            def _(k=k):
                remote(
                    mine.at[across(k)], g1.at[c], s1.at[0], s1.at[1], row_for(k), k
                ).start()

    share(early)
    head = remote(
        e_ref, xin.at[pl.ds(nb + own, own)], hsem.at[0], hsem.at[1], row_at(rows - 1), c
    )
    got1 = g1.at[pl.ds(0, cols - 1)]
    g1[c] = mine[0]

    @pl.when(is_early)
    def _():
        head.start()
        pl.semaphore_wait(colsem, len(late))

        @pl.when(serves)
        def _():
            pl.semaphore_wait(rowsem, rows - 1)
            signal(gosem, r, other)

        share(late)

    @pl.when(is_late)
    def _():
        pl.semaphore_wait(gosem, 1)
        share(late)
        head.start()

    await_bytes(got1, s1.at[1])
    get_plan.wait()
    get_off.wait()

    order = sorted(range(1, rows), key=lambda k: -min(k, rows - k)) + [0]
    for k in order:
        dst = stage.at[k] if k else g2.at[r]
        for j in range(2):
            block = jnp.clip(2 * row_at(k) - 1 + j, 0, blocks - 1)
            dst[2 * part * j : 2 * part * (j + 1)] = g1[plan_ref[0, block]]
    for k in order[:-1]:
        remote(stage.at[k], g2.at[r], s2.at[0], s2.at[1], row_at(k), c).start()

    get_e.wait()
    head.wait_recv()
    off = off_ref[0]
    s0 = xin[pl.ds(off, nb)]

    ri = lax.broadcasted_iota(jnp.int32, (nb, nb), 0)
    ci = lax.broadcasted_iota(jnp.int32, (nb, nb), 1)
    eye = (ri == ci).astype(F32)

    def block_map(j, packed, factor):
        number = 2 * r - 1 + j
        live = ((number >= 0) & (number < blocks)).astype(F32)
        fresh = xin[pl.ds(off + nb * (1 + j), nb)]
        packed = packed.reshape(nb, nb)
        factor = factor.reshape(nb, nb) * live
        lower = jnp.where(ri >= ci, packed, 0.0)
        upper = jnp.where(ri >= ci, 0.0, packed)
        vectors = jnp.concatenate([lower, upper], axis=0)
        tv = mm(factor, vectors, rhs_t=True)
        m, n = tv[:, :nb], tv[:, nb:]
        z = mm(n, fresh)
        w = mm(vectors if j < 2 else lower, jnp.concatenate([m, z], axis=1))
        if j == 2:
            return eye - w[:, :nb], -w[:, nb:]
        return eye - w[:nb, :nb], -w[:nb, nb:], -w[nb:, :nb], fresh - w[nb:, nb:]

    await_bytes(g2.at[pl.ds(0, rows - 1)], s2.at[1])

    third = remote(
        g2.at[:, pl.ds(0, 2 * part)], g3, s3.at[0], s3.at[1], row_at(rows - 1), c
    )
    third.start()
    c0, d0, a0, b0 = block_map(0, g2[:, 0:part], g2[:, part : 2 * part])
    c1, d1, a1, b1 = block_map(1, g2[:, 2 * part : 3 * part], g2[:, 3 * part : 4 * part])
    w = mm(jnp.concatenate([a1, c1], axis=0), jnp.concatenate([a0, b0], axis=1))
    ebuf[0] = w[:nb, :nb]
    ebuf[1] = w[:nb, nb:] + b1

    to_core1 = remote(ebuf, p1buf, psem.at[0], psem.at[1], r ^ 1, c)
    to_pair = remote(fbuf, abuf, asem.at[0], asem.at[1], r ^ 2, c)
    prefix = remote(abuf, pbuf, psem.at[0], psem.at[1], r ^ 1, c)
    state = remote(sbuf, sbuf, dsem.at[0], dsem.at[1], r ^ 1, c)
    core0, core1 = core == 0, core == 1

    @pl.when(core0)
    def _():
        to_core1.start()

    cbuf[0:nb] = c0
    dbuf[0:nb] = d0
    cbuf[nb : 2 * nb] = w[nb:, :nb]
    dbuf[nb : 2 * nb] = w[nb:, nb:] + d1

    @pl.when(core1)
    def _():
        to_core1.wait_recv()
        w = mm(ebuf[0], both(p1buf))
        fbuf[0] = w[:, :nb]
        fbuf[1] = w[:, nb:] + ebuf[1]
        to_pair.start()

    third.wait_recv()
    c2, d2 = block_map(2, g3[:, 0:part], g3[:, part : 2 * part])
    w = mm(c2, both(ebuf))
    cbuf[2 * nb : 3 * nb] = w[:, :nb]
    dbuf[2 * nb : 3 * nb] = w[:, nb:] + d2

    def along_x(step, half):
        return remote(
            hbuf.at[half], bbuf.at[x, half], bsend.at[step, half], brecv.at[x, half],
            lax.rem(r + 4 * step, rows), c,
        )

    @pl.when(core1)
    def _():
        to_pair.wait_recv()
        first = pair == 0

        @pl.when(pair == 1)
        def _():
            prefix.start()

        late_g = jnp.where(first, abuf[0], fbuf[0])
        late_b = jnp.where(first, abuf[1], fbuf[1])
        early_pair = jnp.where(first, both(fbuf), both(abuf))
        w = mm(late_g, early_pair)
        hbuf[0] = w[:, :nb]
        hbuf[1] = w[:, nb:] + late_b
        for step in range(1, groups):
            @pl.when(x + step < groups)
            def _(step=step):
                along_x(step, 1).start()

                @pl.when(x > 0)
                def _():
                    along_x(step, 0).start()

        @pl.when(pair == 0)
        def _():
            pbuf[...] = p1buf[...]

        @pl.when(pair == 1)
        def _():
            w = mm(p1buf[0], both(abuf))
            pbuf[0] = w[:, :nb]
            pbuf[1] = w[:, nb:] + p1buf[1]

    @pl.when(core0 & (pair == 1))
    def _():
        prefix.wait_recv()

    @pl.when(core1 | (pair == 1))
    def _():
        w = mm(cbuf[...], both(pbuf))
        cbuf[...] = w[:, :nb]
        dbuf[...] = w[:, nb:] + dbuf[...]

    @pl.when(x == 0)
    def _():
        sbuf[...] = s0

    @pl.when((x > 0) & core1)
    def _():
        for source in range(groups - 1):
            @pl.when(x > source)
            def _(source=source):
                await_bytes(bbuf.at[source, 1], brecv.at[source, 1])
                if source:
                    await_bytes(bbuf.at[source, 0], brecv.at[source, 0])
                    sbuf[...] = mm(bbuf[source, 0], sbuf[...]) + bbuf[source, 1]
                else:
                    sbuf[...] = bbuf[source, 1]
        state.start()

    @pl.when((x > 0) & core0)
    def _():
        state.wait_recv()

    y_ref[...] = mm(cbuf[...], sbuf[...]) + dbuf[...]

    await_bytes(got1, s1.at[0])
    head.wait_send()
    await_bytes(g2.at[pl.ds(0, rows - 1)], s2.at[0])
    third.wait_send()

    @pl.when(core0)
    def _():
        to_core1.wait_send()

    @pl.when(core1)
    def _():
        to_pair.wait_send()

        @pl.when(pair == 1)
        def _():
            prefix.wait_send()

        @pl.when(x > 0)
        def _():
            state.wait_send()

        for step in range(1, groups):
            @pl.when(x + step < groups)
            def _(step=step):
                along_x(step, 1).wait_send()

                @pl.when(x > 0)
                def _():
                    along_x(step, 0).wait_send()


def solution(mesh):
    rows, cols = mesh.shape["row"], mesh.shape["col"]

    def on_device(eigvecs, offsets, plan, refl_v, refl_t):
        own, width = eigvecs.shape
        nb = refl_t.shape[1]
        part = nb // rows
        dma = pltpu.SemaphoreType.DMA
        square = (nb, nb)
        y = pl.pallas_call(
            functools.partial(kernel, rows, cols),
            out_shape=pltpu.VMEM((3 * nb, width), F32),
            in_specs=[
                pl.BlockSpec(memory_space=pl.ANY),
                pl.BlockSpec(memory_space=pl.ANY),
                pl.BlockSpec(memory_space=pl.ANY),
                pl.BlockSpec(memory_space=pl.ANY),
                pl.BlockSpec(memory_space=pl.ANY),
            ],
            out_specs=pl.BlockSpec(memory_space=pltpu.VMEM),
            scratch_shapes=[
                pltpu.SMEM(offsets.shape, jnp.int32),
                pltpu.SMEM(plan.shape, jnp.int32),
                pltpu.VMEM((nb + 2 * own, width), F32),
                pltpu.VMEM((2, part, nb), F32),
                pltpu.VMEM((2, part, nb), F32),
                pltpu.VMEM((2, 2 * part, nb), F32),
                pltpu.VMEM((cols, 2 * part, nb), F32),
                pltpu.VMEM((rows, 4 * part, nb), F32),
                pltpu.VMEM((rows, 4 * part, nb), F32),
                pltpu.VMEM((rows, 2 * part, nb), F32),
                pltpu.VMEM((2,) + square, F32),
                pltpu.VMEM((2,) + square, F32),
                pltpu.VMEM((2,) + square, F32),
                pltpu.VMEM((2,) + square, F32),
                pltpu.VMEM((2,) + square, F32),
                pltpu.VMEM((rows // 4, 2) + square, F32),
                pltpu.VMEM((2,) + square, F32),
                pltpu.VMEM(square, F32),
                pltpu.VMEM((3 * nb, nb), F32),
                pltpu.VMEM((3 * nb, width), F32),
                dma((3,)), dma((2, 4)), dma((2,)), dma((2,)), dma((2,)), dma((2,)), dma((2,)), dma((2,)),
                dma((rows // 4, 2)), dma((rows // 4, 2)), dma((2,)),
                pltpu.SemaphoreType.REGULAR, pltpu.SemaphoreType.REGULAR,
                pltpu.SemaphoreType.REGULAR,
            ],
            compiler_params=pltpu.CompilerParams(
                collective_id=0, has_side_effects=True, vmem_limit_bytes=60 * 2**20
            ),
            cost_estimate=pl.CostEstimate(
                flops=2 * 30 * nb**3, bytes_accessed=4 * 10 * nb * nb, transcendentals=0
            ),
            name="chase",
        )(offsets, plan, eigvecs, refl_v.transpose(1, 0, 2), refl_t)
        return lax.dynamic_slice(y, (nb - offsets[0], 0), (own, width))

    return jax.shard_map(
        on_device,
        mesh=mesh,
        in_specs=(P("row", "col"), P(), P(), P("col", None, None), P("col", None, None)),
        out_specs=P("row", "col"),
        check_vma=False,
    )
```

```python
import functools

import jax
import jax.numpy as jnp
from jax import lax
from jax.experimental import pallas as pl
from jax.experimental.pallas import tpu as pltpu
from jax.sharding import PartitionSpec as P

MESH = pl.DeviceIdType.MESH
F32 = jnp.float32
BF16 = jnp.bfloat16


def split(a):
    hi = a.astype(BF16)
    return hi, (a - hi.astype(F32)).astype(BF16)


def mm(a, b, rhs_t=False):
    dims = (((1,), (1 if rhs_t else 0,)), ((), ()))
    ah, al = split(a)
    bh, bl = split(b)
    dot = functools.partial(
        lax.dot_general, dimension_numbers=dims, preferred_element_type=F32
    )
    return dot(ah, bl) + dot(al, bh) + dot(ah, bh)


def both(pair):
    return jnp.concatenate([pair[0], pair[1]], axis=1)


def classes(cols):
    if cols == 32:
        start_z = (0.0, 0.9, 1.9, 2.8, 5.8, 6.7, 7.6, 8.4)
        start_y = (0.4, 2.2, 4.7, 3.3)
        start = {4 * z + y: start_z[z] + start_y[y] for z in range(8) for y in range(4)}
        served = {(5, 0): (4, 0), (6, 0): (3, 0), (7, 0): (1, 0), (3, 2): (2, 2)}
        for y in (1, 2, 3):
            served.update({(4 + k, y): (3 - k, y) for k in range(4)})
        served[4, 2] = (2, 2)
        partner = {4 * a + b: 4 * d + e for (a, b), (d, e) in served.items()}
    else:
        start = {k: k for k in range(cols)}
        partner = {k: k - cols // 2 for k in range((cols + 1) // 2, cols)}
    order = sorted(start, key=lambda k: start[k])
    early = [k for k in order if k not in partner]
    return early, [k for k in order if k in partner], partner


def kernel(
    rows, cols, off_hbm, plan_hbm, e_ref, v_ref, t_ref, y_ref,
    off_ref, plan_ref, xin, low, up, mine, g1, stage, g2, g3, ebuf, p1buf, fbuf, abuf, hbuf, bbuf, pbuf, sbuf, cbuf, dbuf,
    lsem, msem, hsem, s1, s2, s3, psem, asem, bsend, brecv, dsem, rowsem, colsem, gosem,
):
    nb = t_ref.shape[1]
    part = nb // rows
    own = e_ref.shape[0]
    r = lax.axis_index("row")
    c = lax.axis_index("col")
    core, pair, x = r % 2, (r // 2) % 2, r // 4
    groups = rows // 4
    early, late, partner = classes(cols)
    blocks = 2 * rows - 2

    is_late = functools.reduce(jnp.logical_or, [c == k for k in late])
    server = sum(jnp.where(c == a, b, 0) for a, b in partner.items())
    is_early = jnp.logical_not(is_late)

    def row_at(k):
        return lax.rem(r + k, rows)

    swaps = cols % 8 == 0

    def across(k):
        return (lax.rem(c - k + 4 * cols, 4) == 2).astype(jnp.int32) if swaps else 0

    def row_for(k):
        return r ^ (2 * across(k))

    def remote(src, dst, send, recv, to_row, to_col):
        return pltpu.make_async_remote_copy(
            src_ref=src, dst_ref=dst, send_sem=send, recv_sem=recv,
            device_id=(to_row, to_col), device_id_type=MESH,
        )

    def signal(sem, to_row, to_col):
        pl.semaphore_signal(sem, 1, device_id=(to_row, to_col), device_id_type=MESH)

    def await_bytes(ref, sem):
        pltpu.make_async_copy(ref, ref, sem).wait()

    mine_parts = []
    for i in range(1 + swaps):
        at = pl.multiple_of((r ^ (2 * i)) * part, part)
        end = jnp.minimum(nb + at + part - 1, 2 * nb - 2)
        mine_parts += [
            pltpu.make_async_copy(v_ref.at[pl.ds(at, part), 0], low.at[i], msem.at[i, 0]),
            pltpu.make_async_copy(
                v_ref.at[pl.ds(nb + at, part - 1), 0],
                up.at[i, pl.ds(0, part - 1)],
                msem.at[i, 1],
            ),
            pltpu.make_async_copy(
                v_ref.at[pl.ds(end, 1), 0], up.at[i, pl.ds(part - 1, 1)], msem.at[i, 2]
            ),
            pltpu.make_async_copy(
                t_ref.at[0, pl.ds(at, part)], mine.at[i, pl.ds(part, part)], msem.at[i, 3]
            ),
        ]
    get_e = pltpu.make_async_copy(e_ref, xin.at[pl.ds(nb, own)], lsem.at[0])
    get_plan = pltpu.make_async_copy(plan_hbm, plan_ref, lsem.at[1])
    get_off = pltpu.make_async_copy(off_hbm, off_ref, lsem.at[2])
    for copy in mine_parts:
        copy.start()

    barrier = pltpu.get_barrier_semaphore()

    @pl.when(is_early)
    def _():
        for k in late[::-1] + early[::-1]:
            @pl.when(c != k)
            def _(k=k):
                signal(barrier, row_for(k), k)
        for k in range(1, rows):
            signal(barrier, row_at(k), c)

        for a, b in partner.items():
            @pl.when(c == b)
            def _(a=a):
                for k in range(1, rows):
                    signal(barrier, row_at(k), a)

    @pl.when(is_late)
    def _():
        pl.semaphore_wait(barrier, len(early) + rows - 1)
        for k in early:
            signal(colsem, row_for(k), k)
        for k in range(1, rows):
            signal(rowsem, row_at(k), server)

    xin[0:nb] = jnp.zeros((nb, nb), F32)
    for copy in mine_parts:
        copy.wait()
    for i in range(1 + swaps):
        at = (r ^ (2 * i)) * part
        row_ids = lax.broadcasted_iota(jnp.int32, (part, nb), 0) + at
        col_ids = lax.broadcasted_iota(jnp.int32, (part, nb), 1)
        mine[i, 0:part] = jnp.where(row_ids >= col_ids, low[i], up[i])

    @pl.when(is_early)
    def _():
        pl.semaphore_wait(barrier, len(early) - 1 + rows - 1)

    def share(to):
        for k in to:
            @pl.when(c != k)
            def _(k=k):
                remote(
                    mine.at[across(k)], g1.at[c], s1.at[0], s1.at[1], row_for(k), k
                ).start()

    share(early)
    for copy in (get_e, get_plan, get_off):
        copy.start()
    head = remote(
        e_ref, xin.at[pl.ds(nb + own, own)], hsem.at[0], hsem.at[1], row_at(rows - 1), c
    )
    got1 = g1.at[pl.ds(0, cols - 1)]
    g1[c] = mine[0]

    @pl.when(is_early)
    def _():
        head.start()
        pl.semaphore_wait(colsem, len(late))
        for b in sorted(set(partner.values())):
            served = [k for k in late if partner[k] == b]

            @pl.when(c == b)
            def _(served=served):
                pl.semaphore_wait(rowsem, (rows - 1) * len(served))
                for a in served:
                    signal(gosem, r, a)

        share(late)

    @pl.when(is_late)
    def _():
        pl.semaphore_wait(gosem, 1)
        share(late)
        head.start()

    await_bytes(got1, s1.at[1])
    get_plan.wait()
    get_off.wait()

    order = sorted(range(1, rows), key=lambda k: -min(k, rows - k)) + [0]
    for k in order:
        dst = stage.at[k] if k else g2.at[r]
        for j in range(2):
            block = jnp.clip(2 * row_at(k) - 1 + j, 0, blocks - 1)
            dst[2 * part * j : 2 * part * (j + 1)] = g1[plan_ref[0, block]]
    for k in order[:-1]:
        remote(stage.at[k], g2.at[r], s2.at[0], s2.at[1], row_at(k), c).start()

    get_e.wait()
    head.wait_recv()
    off = off_ref[0]
    s0 = xin[pl.ds(off, nb)]

    ri = lax.broadcasted_iota(jnp.int32, (nb, nb), 0)
    ci = lax.broadcasted_iota(jnp.int32, (nb, nb), 1)
    eye = (ri == ci).astype(F32)

    def block_map(j, packed, factor):
        number = 2 * r - 1 + j
        live = ((number >= 0) & (number < blocks)).astype(F32)
        fresh = xin[pl.ds(off + nb * (1 + j), nb)]
        packed = packed.reshape(nb, nb)
        factor = factor.reshape(nb, nb) * live
        lower = jnp.where(ri >= ci, packed, 0.0)
        upper = jnp.where(ri >= ci, 0.0, packed)
        vectors = jnp.concatenate([lower, upper], axis=0)
        tv = mm(factor, vectors, rhs_t=True)
        m, n = tv[:, :nb], tv[:, nb:]
        z = mm(n, fresh)
        w = mm(vectors if j < 2 else lower, jnp.concatenate([m, z], axis=1))
        if j == 2:
            return eye - w[:, :nb], -w[:, nb:]
        return eye - w[:nb, :nb], -w[:nb, nb:], -w[nb:, :nb], fresh - w[nb:, nb:]

    await_bytes(g2.at[pl.ds(0, rows - 1)], s2.at[1])

    third = remote(
        g2.at[:, pl.ds(0, 2 * part)], g3, s3.at[0], s3.at[1], row_at(rows - 1), c
    )
    third.start()
    c0, d0, a0, b0 = block_map(0, g2[:, 0:part], g2[:, part : 2 * part])
    c1, d1, a1, b1 = block_map(1, g2[:, 2 * part : 3 * part], g2[:, 3 * part : 4 * part])
    w = mm(jnp.concatenate([a1, c1], axis=0), jnp.concatenate([a0, b0], axis=1))
    ebuf[0] = w[:nb, :nb]
    ebuf[1] = w[:nb, nb:] + b1

    to_core1 = remote(ebuf, p1buf, psem.at[0], psem.at[1], r ^ 1, c)
    to_pair = remote(fbuf, abuf, asem.at[0], asem.at[1], r ^ 2, c)
    prefix = remote(abuf, pbuf, psem.at[0], psem.at[1], r ^ 1, c)
    state = remote(sbuf, sbuf, dsem.at[0], dsem.at[1], r ^ 1, c)
    core0, core1 = core == 0, core == 1

    @pl.when(core0)
    def _():
        to_core1.start()

    cbuf[0:nb] = c0
    dbuf[0:nb] = d0
    cbuf[nb : 2 * nb] = w[nb:, :nb]
    dbuf[nb : 2 * nb] = w[nb:, nb:] + d1

    @pl.when(core1)
    def _():
        to_core1.wait_recv()
        w = mm(ebuf[0], both(p1buf))
        fbuf[0] = w[:, :nb]
        fbuf[1] = w[:, nb:] + ebuf[1]
        to_pair.start()

    def along_x(step, half):
        return remote(
            hbuf.at[half], bbuf.at[x, half], bsend.at[step, half], brecv.at[x, half],
            lax.rem(r + 4 * step, rows), c,
        )

    @pl.when(core1)
    def _():
        to_pair.wait_recv()
        first = pair == 0

        @pl.when(pair == 1)
        def _():
            prefix.start()

        late_g = jnp.where(first, abuf[0], fbuf[0])
        late_b = jnp.where(first, abuf[1], fbuf[1])
        early_pair = jnp.where(first, both(fbuf), both(abuf))
        w = mm(late_g, early_pair)
        hbuf[0] = w[:, :nb]
        hbuf[1] = w[:, nb:] + late_b
        for step in range(1, groups):
            @pl.when(x + step < groups)
            def _(step=step):
                along_x(step, 1).start()

                @pl.when(x > 0)
                def _():
                    along_x(step, 0).start()

    third.wait_recv()
    c2, d2 = block_map(2, g3[:, 0:part], g3[:, part : 2 * part])
    w = mm(c2, both(ebuf))
    cbuf[2 * nb : 3 * nb] = w[:, :nb]
    dbuf[2 * nb : 3 * nb] = w[:, nb:] + d2

    @pl.when(core1 & (pair == 0))
    def _():
        pbuf[...] = p1buf[...]

    @pl.when(core1 & (pair == 1))
    def _():
        w = mm(p1buf[0], both(abuf))
        pbuf[0] = w[:, :nb]
        pbuf[1] = w[:, nb:] + p1buf[1]

    @pl.when(core0 & (pair == 1))
    def _():
        prefix.wait_recv()

    @pl.when(core1 | (pair == 1))
    def _():
        w = mm(cbuf[...], both(pbuf))
        cbuf[...] = w[:, :nb]
        dbuf[...] = w[:, nb:] + dbuf[...]

    @pl.when(x == 0)
    def _():
        sbuf[...] = s0

    @pl.when((x > 0) & core1)
    def _():
        for source in range(groups - 1):
            @pl.when(x > source)
            def _(source=source):
                await_bytes(bbuf.at[source, 1], brecv.at[source, 1])
                if source:
                    await_bytes(bbuf.at[source, 0], brecv.at[source, 0])
                    sbuf[...] = mm(bbuf[source, 0], sbuf[...]) + bbuf[source, 1]
                else:
                    sbuf[...] = bbuf[source, 1]
        state.start()

    @pl.when((x > 0) & core0)
    def _():
        state.wait_recv()

    dbuf[...] = mm(cbuf[...], sbuf[...]) + dbuf[...]
    y_ref[...] = dbuf[pl.ds(nb - off, own)]

    await_bytes(got1, s1.at[0])
    head.wait_send()
    await_bytes(g2.at[pl.ds(0, rows - 1)], s2.at[0])
    third.wait_send()

    @pl.when(core0)
    def _():
        to_core1.wait_send()

    @pl.when(core1)
    def _():
        to_pair.wait_send()

        @pl.when(pair == 1)
        def _():
            prefix.wait_send()

        @pl.when(x > 0)
        def _():
            state.wait_send()

        for step in range(1, groups):
            @pl.when(x + step < groups)
            def _(step=step):
                along_x(step, 1).wait_send()

                @pl.when(x > 0)
                def _():
                    along_x(step, 0).wait_send()


def solution(mesh):
    rows, cols = mesh.shape["row"], mesh.shape["col"]

    def on_device(eigvecs, offsets, plan, refl_v, refl_t):
        own, width = eigvecs.shape
        nb = refl_t.shape[1]
        part = nb // rows
        dma = pltpu.SemaphoreType.DMA
        square = (nb, nb)
        y = pl.pallas_call(
            functools.partial(kernel, rows, cols),
            out_shape=pltpu.VMEM((own, width), F32),
            in_specs=[
                pl.BlockSpec(memory_space=pl.ANY),
                pl.BlockSpec(memory_space=pl.ANY),
                pl.BlockSpec(memory_space=pl.ANY),
                pl.BlockSpec(memory_space=pl.ANY),
                pl.BlockSpec(memory_space=pl.ANY),
            ],
            out_specs=pl.BlockSpec(memory_space=pltpu.VMEM),
            scratch_shapes=[
                pltpu.SMEM(offsets.shape, jnp.int32),
                pltpu.SMEM(plan.shape, jnp.int32),
                pltpu.VMEM((nb + 2 * own, width), F32),
                pltpu.VMEM((2, part, nb), F32),
                pltpu.VMEM((2, part, nb), F32),
                pltpu.VMEM((2, 2 * part, nb), F32),
                pltpu.VMEM((cols, 2 * part, nb), F32),
                pltpu.VMEM((rows, 4 * part, nb), F32),
                pltpu.VMEM((rows, 4 * part, nb), F32),
                pltpu.VMEM((rows, 2 * part, nb), F32),
                pltpu.VMEM((2,) + square, F32),
                pltpu.VMEM((2,) + square, F32),
                pltpu.VMEM((2,) + square, F32),
                pltpu.VMEM((2,) + square, F32),
                pltpu.VMEM((2,) + square, F32),
                pltpu.VMEM((rows // 4, 2) + square, F32),
                pltpu.VMEM((2,) + square, F32),
                pltpu.VMEM(square, F32),
                pltpu.VMEM((3 * nb, nb), F32),
                pltpu.VMEM((3 * nb, width), F32),
                dma((3,)), dma((2, 4)), dma((2,)), dma((2,)), dma((2,)), dma((2,)), dma((2,)), dma((2,)),
                dma((rows // 4, 2)), dma((rows // 4, 2)), dma((2,)),
                pltpu.SemaphoreType.REGULAR, pltpu.SemaphoreType.REGULAR,
                pltpu.SemaphoreType.REGULAR,
            ],
            compiler_params=pltpu.CompilerParams(
                collective_id=0, has_side_effects=True, vmem_limit_bytes=60 * 2**20
            ),
            cost_estimate=pl.CostEstimate(
                flops=2 * 30 * nb**3, bytes_accessed=4 * 10 * nb * nb, transcendentals=0
            ),
            name="chase",
        )(offsets, plan, eigvecs, refl_v.transpose(1, 0, 2), refl_t)
        return y

    return jax.shard_map(
        on_device,
        mesh=mesh,
        in_specs=(P("row", "col"), P(), P(), P("col", None, None), P("col", None, None)),
        out_specs=P("row", "col"),
        check_vma=False,
    )
```

```python
import functools

import jax
import jax.numpy as jnp
from jax import lax
from jax.experimental import pallas as pl
from jax.experimental.pallas import tpu as pltpu
from jax.sharding import PartitionSpec as P

MESH = pl.DeviceIdType.MESH
F32 = jnp.float32
BF16 = jnp.bfloat16


def split(a):
    hi = a.astype(BF16)
    return hi, (a - hi.astype(F32)).astype(BF16)


def mm(a, b, rhs_t=False):
    dims = (((1,), (1 if rhs_t else 0,)), ((), ()))
    ah, al = split(a)
    bh, bl = split(b)
    dot = functools.partial(
        lax.dot_general, dimension_numbers=dims, preferred_element_type=F32
    )
    return dot(ah, bl) + dot(al, bh) + dot(ah, bh)


def both(pair):
    return jnp.concatenate([pair[0], pair[1]], axis=1)


def classes(cols):
    if cols == 32:
        start_z = (0.0, 0.9, 1.9, 2.8, 5.8, 6.7, 7.6, 8.4)
        start_y = (0.4, 2.2, 4.7, 3.3)
        start = {4 * z + y: start_z[z] + start_y[y] for z in range(8) for y in range(4)}
        served = {(5, 0): (4, 0), (6, 0): (3, 0), (7, 0): (1, 0), (3, 2): (2, 2)}
        for y in (1, 2, 3):
            served.update({(4 + k, y): (3 - k, y) for k in range(4)})
        served[4, 2] = (2, 2)
        partner = {4 * a + b: 4 * d + e for (a, b), (d, e) in served.items()}
    else:
        start = {k: k for k in range(cols)}
        partner = {k: k - cols // 2 for k in range((cols + 1) // 2, cols)}
    order = sorted(start, key=lambda k: start[k])
    early = [k for k in order if k not in partner]
    return early, [k for k in order if k in partner], partner


def kernel(
    rows, cols, off_hbm, plan_hbm, e_ref, v_ref, t_ref, y_ref,
    off_ref, plan_ref, xin, low, up, mine, g1, stage, g2, g3, ebuf, p1buf, fbuf, abuf, hbuf, bbuf, pbuf, sbuf, cbuf, dbuf,
    lsem, msem, hsem, s1, s2, s3, esem, psem, asem, bsend, brecv, dsem, rowsem, colsem, gosem,
):
    nb = t_ref.shape[1]
    part = nb // rows
    own = e_ref.shape[0]
    r = lax.axis_index("row")
    c = lax.axis_index("col")
    core, pair, x = r % 2, (r // 2) % 2, r // 4
    groups = rows // 4
    early, late, partner = classes(cols)
    blocks = 2 * rows - 2

    is_late = functools.reduce(jnp.logical_or, [c == k for k in late])
    server = sum(jnp.where(c == a, b, 0) for a, b in partner.items())
    is_early = jnp.logical_not(is_late)

    def row_at(k):
        return lax.rem(r + k, rows)

    swaps = cols % 8 == 0

    def across(k):
        return (lax.rem(c - k + 4 * cols, 4) == 2).astype(jnp.int32) if swaps else 0

    def row_for(k):
        return r ^ (2 * across(k))

    def remote(src, dst, send, recv, to_row, to_col):
        return pltpu.make_async_remote_copy(
            src_ref=src, dst_ref=dst, send_sem=send, recv_sem=recv,
            device_id=(to_row, to_col), device_id_type=MESH,
        )

    def signal(sem, to_row, to_col):
        pl.semaphore_signal(sem, 1, device_id=(to_row, to_col), device_id_type=MESH)

    def await_bytes(ref, sem):
        pltpu.make_async_copy(ref, ref, sem).wait()

    mine_parts = []
    for i in range(1 + swaps):
        at = pl.multiple_of((r ^ (2 * i)) * part, part)
        end = jnp.minimum(nb + at + part - 1, 2 * nb - 2)
        mine_parts += [
            pltpu.make_async_copy(v_ref.at[pl.ds(at, part), 0], low.at[i], msem.at[i, 0]),
            pltpu.make_async_copy(
                v_ref.at[pl.ds(nb + at, part - 1), 0],
                up.at[i, pl.ds(0, part - 1)],
                msem.at[i, 1],
            ),
            pltpu.make_async_copy(
                v_ref.at[pl.ds(end, 1), 0], up.at[i, pl.ds(part - 1, 1)], msem.at[i, 2]
            ),
            pltpu.make_async_copy(
                t_ref.at[0, pl.ds(at, part)], mine.at[i, pl.ds(part, part)], msem.at[i, 3]
            ),
        ]
    get_e = pltpu.make_async_copy(e_ref, xin.at[pl.ds(own, own)], lsem.at[0])
    get_plan = pltpu.make_async_copy(plan_hbm, plan_ref, lsem.at[1])
    get_off = pltpu.make_async_copy(off_hbm, off_ref, lsem.at[2])
    for copy in mine_parts:
        copy.start()

    barrier = pltpu.get_barrier_semaphore()

    @pl.when(is_early)
    def _():
        for k in late[::-1] + early[::-1]:
            @pl.when(c != k)
            def _(k=k):
                signal(barrier, row_for(k), k)
        for k in range(1, rows):
            signal(barrier, row_at(k), c)

        for a, b in partner.items():
            @pl.when(c == b)
            def _(a=a):
                for k in range(1, rows):
                    signal(barrier, row_at(k), a)

    @pl.when(is_late)
    def _():
        pl.semaphore_wait(barrier, len(early) + rows - 1)
        for k in early:
            signal(colsem, row_for(k), k)
        for k in range(1, rows):
            signal(rowsem, row_at(k), server)

    @pl.when(core == 0)
    def _():
        xin[own - nb : own] = jnp.zeros((nb, nb), F32)

    for copy in mine_parts:
        copy.wait()
    for i in range(1 + swaps):
        at = (r ^ (2 * i)) * part
        row_ids = lax.broadcasted_iota(jnp.int32, (part, nb), 0) + at
        col_ids = lax.broadcasted_iota(jnp.int32, (part, nb), 1)
        mine[i, 0:part] = jnp.where(row_ids >= col_ids, low[i], up[i])

    @pl.when(is_early)
    def _():
        pl.semaphore_wait(barrier, len(early) - 1 + rows - 1)

    def share(to):
        for k in to:
            @pl.when(c != k)
            def _(k=k):
                remote(
                    mine.at[across(k)], g1.at[c], s1.at[0], s1.at[1], row_for(k), k
                ).start()

    share(early)
    for copy in (get_e, get_plan, get_off):
        copy.start()
    head = remote(
        e_ref, xin.at[pl.ds(2 * own, own)], hsem.at[0], hsem.at[1], row_at(rows - 1), c
    )
    tail = remote(e_ref, xin.at[pl.ds(0, own)], hsem.at[2], hsem.at[3], r ^ 1, c)

    def send_rows():
        head.start()

        @pl.when(core == 0)
        def _():
            tail.start()

    got1 = g1.at[pl.ds(0, cols - 1)]
    g1[c] = mine[0]

    @pl.when(is_early)
    def _():
        send_rows()
        pl.semaphore_wait(colsem, len(late))
        for b in sorted(set(partner.values())):
            served = [k for k in late if partner[k] == b]

            @pl.when(c == b)
            def _(served=served):
                pl.semaphore_wait(rowsem, (rows - 1) * len(served))
                for a in served:
                    signal(gosem, r, a)

        share(late)

    @pl.when(is_late)
    def _():
        pl.semaphore_wait(gosem, 1)
        share(late)
        send_rows()

    await_bytes(got1, s1.at[1])
    get_plan.wait()
    get_off.wait()

    chips = rows // 2
    chip = r // 2
    core0, core1 = core == 0, core == 1
    order = sorted(range(1, chips), key=lambda k: -min(k, chips - k)) + [0]

    def to_chip(k):
        to = 2 * lax.rem(chip + k, chips) + 1
        return remote(stage.at[k], g2.at[r], s2.at[0], s2.at[1], to, c)

    for k in order:
        for j in range(4):
            block = jnp.clip(4 * lax.rem(chip + k, chips) - 1 + j, 0, blocks - 1)
            stage[k, 2 * part * j : 2 * part * (j + 1)] = g1[plan_ref[0, block]]
    for k in order[:-1]:
        to_chip(k).start()

    @pl.when(core0)
    def _():
        to_chip(0).start()

    @pl.when(core1)
    def _():
        g2[r] = stage[0]
        tail.wait_recv()

    get_e.wait()
    head.wait_recv()
    off = off_ref[0]
    s0 = xin[pl.ds(off + own - nb, nb)]

    ri = lax.broadcasted_iota(jnp.int32, (nb, nb), 0)
    ci = lax.broadcasted_iota(jnp.int32, (nb, nb), 1)
    eye = (ri == ci).astype(F32)

    def triangles(packed):
        packed = packed.reshape(nb, nb)
        return jnp.where(ri >= ci, packed, 0.0), jnp.where(ri >= ci, 0.0, packed)

    def fresh(n):
        return xin[pl.ds(off + own + nb * (n + 1), nb)]

    def entry(j):
        lo = 2 * part * j
        return g2[:, lo : lo + part], g2[:, lo + part : lo + 2 * part]

    def middle(n, packed, factor):
        live = ((2 * r + n >= 0) & (2 * r + n < blocks)).astype(F32)
        vectors = jnp.concatenate(triangles(packed), axis=0)
        tv = mm(factor.reshape(nb, nb) * live, vectors, rhs_t=True)
        return jnp.concatenate([tv[:, :nb], mm(tv[:, nb:], fresh(n))], axis=1)

    def passed(n, packed, mid):
        w = mm(triangles(packed)[1], mid)
        return -w[:, :nb], fresh(n) - w[:, nb:]

    def done(packed, mid):
        w = mm(triangles(packed)[0], mid)
        return eye - w[:, :nb], -w[:, nb:]

    entries = remote(
        g2.at[:, pl.ds(0, 6 * part)], g2.at[:, pl.ds(0, 6 * part)],
        esem.at[0], esem.at[1], r ^ 1, c,
    )
    third = remote(
        g2.at[:, pl.ds(0, 2 * part)], g3, s3.at[0], s3.at[1], row_at(rows - 2), c
    )
    to_pair = remote(fbuf, abuf, asem.at[0], asem.at[1], r ^ 2, c)
    prefix = remote(abuf, pbuf, psem.at[0], psem.at[1], r ^ 1, c)
    state = remote(sbuf, sbuf, dsem.at[0], dsem.at[1], r ^ 1, c)

    @pl.when(core1)
    def _():
        await_bytes(g2.at[pl.ds(0, rows - 1)], s2.at[1])
        entries.start()
        mids = [middle(j - 3, *entry(j)) for j in range(4)]
        (a0, b0), (a1, b1), (a2, b2), (a3, b3) = [
            passed(j - 3, entry(j)[0], mids[j]) for j in range(4)
        ]
        first = mm(a1, jnp.concatenate([a0, b0], axis=1))
        p1buf[0] = first[:, :nb]
        p1buf[1] = first[:, nb:] + b1
        second = mm(a3, jnp.concatenate([a2, b2], axis=1))
        ebuf[0] = second[:, :nb]
        ebuf[1] = second[:, nb:] + b3
        w = mm(ebuf[0], both(p1buf))
        fbuf[0] = w[:, :nb]
        fbuf[1] = w[:, nb:] + ebuf[1]
        to_pair.start()
        third.start()
        c2, d2 = done(entry(2)[0], mids[2])
        cbuf[0:nb] = c2
        dbuf[0:nb] = d2
        c3, d3 = done(entry(3)[0], mids[3])
        w = mm(c3, jnp.concatenate([a2, b2], axis=1))
        cbuf[nb : 2 * nb] = w[:, :nb]
        dbuf[nb : 2 * nb] = w[:, nb:] + d3

    @pl.when(core0)
    def _():
        await_bytes(g2.at[:, pl.ds(0, 6 * part)], esem.at[1])
        mids = [middle(j - 1, *entry(j)) for j in range(3)]
        (a0, b0), (a1, b1) = [passed(j - 1, entry(j)[0], mids[j]) for j in range(2)]
        (c0, d0), (c1, d1), (c2, d2) = [done(entry(j)[0], mids[j]) for j in range(3)]
        cbuf[0:nb] = c0
        dbuf[0:nb] = d0
        w = mm(jnp.concatenate([a1, c1], axis=0), jnp.concatenate([a0, b0], axis=1))
        cbuf[nb : 2 * nb] = w[nb:, :nb]
        dbuf[nb : 2 * nb] = w[nb:, nb:] + d1
        g, b = w[:nb, :nb], w[:nb, nb:] + b1
        w = mm(c2, jnp.concatenate([g, b], axis=1))
        cbuf[2 * nb : 3 * nb] = w[:, :nb]
        dbuf[2 * nb : 3 * nb] = w[:, nb:] + d2

    def along_x(step, half):
        return remote(
            hbuf.at[half], bbuf.at[x, half], bsend.at[step, half], brecv.at[x, half],
            lax.rem(r + 4 * step, rows), c,
        )

    @pl.when(core1)
    def _():
        to_pair.wait_recv()
        first = pair == 0

        @pl.when(pair == 1)
        def _():
            prefix.start()

        late_g = jnp.where(first, abuf[0], fbuf[0])
        late_b = jnp.where(first, abuf[1], fbuf[1])
        early_pair = jnp.where(first, both(fbuf), both(abuf))
        w = mm(late_g, early_pair)
        hbuf[0] = w[:, :nb]
        hbuf[1] = w[:, nb:] + late_b
        for step in range(1, groups):
            @pl.when(x + step < groups)
            def _(step=step):
                along_x(step, 1).start()

                @pl.when(x > 0)
                def _():
                    along_x(step, 0).start()

    @pl.when(core1)
    def _():
        third.wait_recv()
        packed = g3[:, 0:part]
        c4, d4 = done(packed, middle(1, packed, g3[:, part : 2 * part]))
        w = mm(c4, both(ebuf))
        cbuf[2 * nb : 3 * nb] = w[:, :nb]
        dbuf[2 * nb : 3 * nb] = w[:, nb:] + d4

    @pl.when(core1 & (pair == 0))
    def _():
        pbuf[...] = p1buf[...]

    @pl.when(core1 & (pair == 1))
    def _():
        w = mm(p1buf[0], both(abuf))
        pbuf[0] = w[:, :nb]
        pbuf[1] = w[:, nb:] + p1buf[1]

    @pl.when(core0 & (pair == 1))
    def _():
        prefix.wait_recv()

    @pl.when(core1 | (pair == 1))
    def _():
        w = mm(cbuf[...], both(pbuf))
        cbuf[...] = w[:, :nb]
        dbuf[...] = w[:, nb:] + dbuf[...]

    @pl.when(x == 0)
    def _():
        sbuf[...] = s0

    @pl.when((x > 0) & core1)
    def _():
        for source in range(groups - 1):
            @pl.when(x > source)
            def _(source=source):
                await_bytes(bbuf.at[source, 1], brecv.at[source, 1])
                if source:
                    await_bytes(bbuf.at[source, 0], brecv.at[source, 0])
                    sbuf[...] = mm(bbuf[source, 0], sbuf[...]) + bbuf[source, 1]
                else:
                    sbuf[...] = bbuf[source, 1]
        state.start()

    @pl.when((x > 0) & core0)
    def _():
        state.wait_recv()

    dbuf[...] = mm(cbuf[...], sbuf[...]) + dbuf[...]
    y_ref[...] = dbuf[pl.ds(nb - off, own)]

    await_bytes(got1, s1.at[0])
    head.wait_send()
    await_bytes(stage.at[pl.ds(0, chips - 1)], s2.at[0])

    @pl.when(core0)
    def _():
        await_bytes(stage.at[0], s2.at[0])
        tail.wait_send()

    @pl.when(core1)
    def _():
        entries.wait_send()
        third.wait_send()
        to_pair.wait_send()

        @pl.when(pair == 1)
        def _():
            prefix.wait_send()

        @pl.when(x > 0)
        def _():
            state.wait_send()

        for step in range(1, groups):
            @pl.when(x + step < groups)
            def _(step=step):
                along_x(step, 1).wait_send()

                @pl.when(x > 0)
                def _():
                    along_x(step, 0).wait_send()


def solution(mesh):
    rows, cols = mesh.shape["row"], mesh.shape["col"]

    def on_device(eigvecs, offsets, plan, refl_v, refl_t):
        own, width = eigvecs.shape
        nb = refl_t.shape[1]
        part = nb // rows
        dma = pltpu.SemaphoreType.DMA
        square = (nb, nb)
        y = pl.pallas_call(
            functools.partial(kernel, rows, cols),
            out_shape=pltpu.VMEM((own, width), F32),
            in_specs=[
                pl.BlockSpec(memory_space=pl.ANY),
                pl.BlockSpec(memory_space=pl.ANY),
                pl.BlockSpec(memory_space=pl.ANY),
                pl.BlockSpec(memory_space=pl.ANY),
                pl.BlockSpec(memory_space=pl.ANY),
            ],
            out_specs=pl.BlockSpec(memory_space=pltpu.VMEM),
            scratch_shapes=[
                pltpu.SMEM(offsets.shape, jnp.int32),
                pltpu.SMEM(plan.shape, jnp.int32),
                pltpu.VMEM((3 * own, width), F32),
                pltpu.VMEM((2, part, nb), F32),
                pltpu.VMEM((2, part, nb), F32),
                pltpu.VMEM((2, 2 * part, nb), F32),
                pltpu.VMEM((cols, 2 * part, nb), F32),
                pltpu.VMEM((rows // 2, 8 * part, nb), F32),
                pltpu.VMEM((rows, 8 * part, nb), F32),
                pltpu.VMEM((rows, 2 * part, nb), F32),
                pltpu.VMEM((2,) + square, F32),
                pltpu.VMEM((2,) + square, F32),
                pltpu.VMEM((2,) + square, F32),
                pltpu.VMEM((2,) + square, F32),
                pltpu.VMEM((2,) + square, F32),
                pltpu.VMEM((rows // 4, 2) + square, F32),
                pltpu.VMEM((2,) + square, F32),
                pltpu.VMEM(square, F32),
                pltpu.VMEM((3 * nb, nb), F32),
                pltpu.VMEM((3 * nb, width), F32),
                dma((3,)), dma((2, 4)), dma((4,)), dma((2,)), dma((2,)), dma((2,)), dma((2,)), dma((2,)), dma((2,)),
                dma((rows // 4, 2)), dma((rows // 4, 2)), dma((2,)),
                pltpu.SemaphoreType.REGULAR, pltpu.SemaphoreType.REGULAR,
                pltpu.SemaphoreType.REGULAR,
            ],
            compiler_params=pltpu.CompilerParams(
                collective_id=0, has_side_effects=True, vmem_limit_bytes=60 * 2**20
            ),
            cost_estimate=pl.CostEstimate(
                flops=2 * 30 * nb**3, bytes_accessed=4 * 10 * nb * nb, transcendentals=0
            ),
            name="chase",
        )(offsets, plan, eigvecs, refl_v.transpose(1, 0, 2), refl_t)
        return y

    return jax.shard_map(
        on_device,
        mesh=mesh,
        in_specs=(P("row", "col"), P(), P(), P("col", None, None), P("col", None, None)),
        out_specs=P("row", "col"),
        check_vma=False,
    )
```

```python
import functools

import jax
import jax.numpy as jnp
from jax import lax
from jax.experimental import pallas as pl
from jax.experimental.pallas import tpu as pltpu
from jax.sharding import PartitionSpec as P

MESH = pl.DeviceIdType.MESH
F32 = jnp.float32
BF16 = jnp.bfloat16


def split(a):
    hi = a.astype(BF16)
    return hi, (a - hi.astype(F32)).astype(BF16)


def mm(a, b, rhs_t=False):
    ah, al = split(a)
    bh, bl = split(b)
    dot = functools.partial(
        lax.dot_general,
        dimension_numbers=(((1,), (1 if rhs_t else 0,)), ((), ())),
        preferred_element_type=F32,
    )
    if rhs_t:
        return dot(ah, bl) + dot(al, bh) + dot(ah, bh)
    return dot(ah, bl) + dot(
        jnp.concatenate([ah, al], axis=1), jnp.concatenate([bh, bh], axis=0)
    )


def both(pair):
    return jnp.concatenate([pair[0], pair[1]], axis=1)


def classes(cols):
    if cols == 32:
        start_z = (0.0, 0.9, 1.9, 2.8, 5.8, 6.7, 7.6, 8.4)
        start_y = (0.4, 2.2, 4.7, 3.3)
        start = {4 * z + y: start_z[z] + start_y[y] for z in range(8) for y in range(4)}
        served = {(5, 0): (4, 0), (6, 0): (3, 0), (7, 0): (1, 0), (3, 2): (2, 2)}
        for y in (1, 2, 3):
            served.update({(4 + k, y): (3 - k, y) for k in range(4)})
        served[4, 2] = (2, 2)
        partner = {4 * a + b: 4 * d + e for (a, b), (d, e) in served.items()}
    else:
        start = {k: k for k in range(cols)}
        partner = {k: k - cols // 2 for k in range((cols + 1) // 2, cols)}
    order = sorted(start, key=lambda k: start[k])
    early = [k for k in order if k not in partner]
    return early, [k for k in order if k in partner], partner


def kernel(
    rows, cols, off_hbm, plan_hbm, e_ref, v_ref, t_ref, y_ref,
    off_ref, plan_ref, xin, xt, low, up, mine, g1, stage, g2, g3, ebuf, p1buf, fbuf, abuf, hbuf, bbuf, pbuf, sbuf, cbuf, dbuf,
    lsem, msem, hsem, s1, s2, s3, esem, psem, asem, bsend, brecv, dsem, rowsem, colsem, gosem,
):
    nb = t_ref.shape[1]
    part = nb // rows
    own = e_ref.shape[0]
    r = lax.axis_index("row")
    c = lax.axis_index("col")
    core, pair, x = r % 2, (r // 2) % 2, r // 4
    groups = rows // 4
    early, late, partner = classes(cols)
    blocks = 2 * rows - 2

    is_late = functools.reduce(jnp.logical_or, [c == k for k in late])
    server = sum(jnp.where(c == a, b, 0) for a, b in partner.items())
    is_early = jnp.logical_not(is_late)

    def row_at(k):
        return lax.rem(r + k, rows)

    swaps = cols % 8 == 0

    def across(k):
        return (lax.rem(c - k + 4 * cols, 4) == 2).astype(jnp.int32) if swaps else 0

    def row_for(k):
        return r ^ (2 * across(k))

    def remote(src, dst, send, recv, to_row, to_col):
        return pltpu.make_async_remote_copy(
            src_ref=src, dst_ref=dst, send_sem=send, recv_sem=recv,
            device_id=(to_row, to_col), device_id_type=MESH,
        )

    def signal(sem, to_row, to_col):
        pl.semaphore_signal(sem, 1, device_id=(to_row, to_col), device_id_type=MESH)

    def await_bytes(ref, sem):
        pltpu.make_async_copy(ref, ref, sem).wait()

    mine_parts = []
    for i in range(1 + swaps):
        at = pl.multiple_of((r ^ (2 * i)) * part, part)
        end = jnp.minimum(nb + at + part - 1, 2 * nb - 2)
        mine_parts += [
            pltpu.make_async_copy(v_ref.at[pl.ds(at, part), 0], low.at[i], msem.at[i, 0]),
            pltpu.make_async_copy(
                v_ref.at[pl.ds(nb + at, part - 1), 0],
                up.at[i, pl.ds(0, part - 1)],
                msem.at[i, 1],
            ),
            pltpu.make_async_copy(
                v_ref.at[pl.ds(end, 1), 0], up.at[i, pl.ds(part - 1, 1)], msem.at[i, 2]
            ),
            pltpu.make_async_copy(
                t_ref.at[0, pl.ds(at, part)], mine.at[i, pl.ds(part, part)], msem.at[i, 3]
            ),
        ]
    get_e = pltpu.make_async_copy(e_ref, xin.at[pl.ds(own, own)], lsem.at[0])
    get_plan = pltpu.make_async_copy(plan_hbm, plan_ref, lsem.at[1])
    get_off = pltpu.make_async_copy(off_hbm, off_ref, lsem.at[2])
    for copy in mine_parts:
        copy.start()

    barrier = pltpu.get_barrier_semaphore()

    @pl.when(is_early)
    def _():
        for k in late[::-1] + early[::-1]:
            @pl.when(c != k)
            def _(k=k):
                signal(barrier, row_for(k), k)
        for k in range(1, rows):
            signal(barrier, row_at(k), c)

        for a, b in partner.items():
            @pl.when(c == b)
            def _(a=a):
                for k in range(1, rows):
                    signal(barrier, row_at(k), a)

    @pl.when(is_late)
    def _():
        pl.semaphore_wait(barrier, len(early) + rows - 1)
        for k in early:
            signal(colsem, row_for(k), k)
        for k in range(1, rows):
            signal(rowsem, row_at(k), server)

    @pl.when(core == 0)
    def _():
        xin[own - nb : own] = jnp.zeros((nb, nb), F32)

    for copy in mine_parts:
        copy.wait()
    for i in range(1 + swaps):
        at = (r ^ (2 * i)) * part
        row_ids = lax.broadcasted_iota(jnp.int32, (part, nb), 0) + at
        col_ids = lax.broadcasted_iota(jnp.int32, (part, nb), 1)
        mine[i, 0:part] = jnp.where(row_ids >= col_ids, low[i], up[i])

    @pl.when(is_early)
    def _():
        pl.semaphore_wait(barrier, len(early) - 1 + rows - 1)

    def share(to):
        for k in to:
            @pl.when(c != k)
            def _(k=k):
                remote(
                    mine.at[across(k)], g1.at[c], s1.at[0], s1.at[1], row_for(k), k
                ).start()

    share(early)
    for copy in (get_e, get_plan, get_off):
        copy.start()
    head = remote(
        e_ref, xin.at[pl.ds(2 * own, own)], hsem.at[0], hsem.at[1], row_at(rows - 1), c
    )
    tail = remote(e_ref, xin.at[pl.ds(0, own)], hsem.at[2], hsem.at[3], r ^ 1, c)

    def send_rows():
        head.start()

        @pl.when(core == 0)
        def _():
            tail.start()

    got1 = g1.at[pl.ds(0, cols - 1)]
    g1[c] = mine[0]

    @pl.when(is_early)
    def _():
        send_rows()
        pl.semaphore_wait(colsem, len(late))
        for b in sorted(set(partner.values())):
            served = [k for k in late if partner[k] == b]

            @pl.when(c == b)
            def _(served=served):
                pl.semaphore_wait(rowsem, (rows - 1) * len(served))
                for a in served:
                    signal(gosem, r, a)

        share(late)

    @pl.when(is_late)
    def _():
        pl.semaphore_wait(gosem, 1)
        share(late)
        send_rows()

    await_bytes(got1, s1.at[1])
    get_plan.wait()
    get_off.wait()

    chips = rows // 2
    chip = r // 2
    core0, core1 = core == 0, core == 1
    order = sorted(range(1, chips), key=lambda k: -min(k, chips - k)) + [0]

    def to_chip(k):
        to = 2 * lax.rem(chip + k, chips) + 1
        return remote(stage.at[k], g2.at[r], s2.at[0], s2.at[1], to, c)

    for k in order:
        for j in range(4):
            block = jnp.clip(4 * lax.rem(chip + k, chips) - 1 + j, 0, blocks - 1)
            stage[k, 2 * part * j : 2 * part * (j + 1)] = g1[plan_ref[0, block]]
    for k in order[:-1]:
        to_chip(k).start()

    @pl.when(core0)
    def _():
        to_chip(0).start()

    @pl.when(core1)
    def _():
        g2[r] = stage[0]
        tail.wait_recv()

    get_e.wait()
    head.wait_recv()
    off = off_ref[0]
    s0 = xin[pl.ds(off + own - nb, nb)]

    ri = lax.broadcasted_iota(jnp.int32, (nb, nb), 0)
    ci = lax.broadcasted_iota(jnp.int32, (nb, nb), 1)
    eye = (ri == ci).astype(F32)

    def triangles(packed):
        packed = packed.reshape(nb, nb)
        return jnp.where(ri >= ci, packed, 0.0), jnp.where(ri >= ci, 0.0, packed)

    def fresh(n):
        return xin[pl.ds(off + own + nb * (n + 1), nb)]

    def entry(j):
        lo = 2 * part * j
        return g2[:, lo : lo + part], g2[:, lo + part : lo + 2 * part]

    def keep_transposed(blocks_of):
        for n in blocks_of:
            xt[n + 3] = fresh(n).T

    def live(n, factor):
        inside = ((2 * r + n >= 0) & (2 * r + n < blocks)).astype(F32)
        return factor.reshape(nb, nb) * inside

    def sides(n, lower, upper):
        return jnp.concatenate([lower, mm(xt[n + 3], upper)], axis=0)

    def passed(n, packed, factor):
        lower, upper = triangles(packed)
        w = mm(mm(upper, live(n, factor)), sides(n, lower, upper), rhs_t=True)
        return -w[:, :nb], fresh(n) - w[:, nb:]

    def done(n, packed, factor):
        lower, upper = triangles(packed)
        w = mm(mm(lower, live(n, factor)), sides(n, lower, upper), rhs_t=True)
        return eye - w[:, :nb], -w[:, nb:]

    entries = remote(
        g2.at[:, pl.ds(0, 6 * part)], g2.at[:, pl.ds(0, 6 * part)],
        esem.at[0], esem.at[1], r ^ 1, c,
    )
    third = remote(
        g2.at[:, pl.ds(0, 2 * part)], g3, s3.at[0], s3.at[1], row_at(rows - 2), c
    )
    to_pair = remote(fbuf, abuf, asem.at[0], asem.at[1], r ^ 2, c)
    prefix = remote(abuf, pbuf, psem.at[0], psem.at[1], r ^ 1, c)
    state = remote(sbuf, sbuf, dsem.at[0], dsem.at[1], r ^ 1, c)

    @pl.when(core1)
    def _():
        keep_transposed(range(-3, 2))
        await_bytes(g2.at[pl.ds(0, rows - 1)], s2.at[1])
        third.start()
        entries.start()
        (a0, b0), (a1, b1), (a2, b2), (a3, b3) = [
            passed(j - 3, *entry(j)) for j in range(4)
        ]
        first = mm(a1, jnp.concatenate([a0, b0], axis=1))
        p1buf[0] = first[:, :nb]
        p1buf[1] = first[:, nb:] + b1
        second = mm(a3, jnp.concatenate([a2, b2], axis=1))
        ebuf[0] = second[:, :nb]
        ebuf[1] = second[:, nb:] + b3
        w = mm(ebuf[0], both(p1buf))
        fbuf[0] = w[:, :nb]
        fbuf[1] = w[:, nb:] + ebuf[1]
        to_pair.start()
        c2, d2 = done(-1, *entry(2))
        cbuf[0:nb] = c2
        dbuf[0:nb] = d2
        c3, d3 = done(0, *entry(3))
        w = mm(c3, jnp.concatenate([a2, b2], axis=1))
        cbuf[nb : 2 * nb] = w[:, :nb]
        dbuf[nb : 2 * nb] = w[:, nb:] + d3

    @pl.when(core0)
    def _():
        keep_transposed(range(-1, 2))
        await_bytes(g2.at[:, pl.ds(0, 6 * part)], esem.at[1])
        (a0, b0), (a1, b1) = [passed(j - 1, *entry(j)) for j in range(2)]
        (c0, d0), (c1, d1), (c2, d2) = [done(j - 1, *entry(j)) for j in range(3)]
        cbuf[0:nb] = c0
        dbuf[0:nb] = d0
        w = mm(jnp.concatenate([a1, c1], axis=0), jnp.concatenate([a0, b0], axis=1))
        cbuf[nb : 2 * nb] = w[nb:, :nb]
        dbuf[nb : 2 * nb] = w[nb:, nb:] + d1
        g, b = w[:nb, :nb], w[:nb, nb:] + b1
        w = mm(c2, jnp.concatenate([g, b], axis=1))
        cbuf[2 * nb : 3 * nb] = w[:, :nb]
        dbuf[2 * nb : 3 * nb] = w[:, nb:] + d2

    def along_x(step, half):
        return remote(
            hbuf.at[half], bbuf.at[x, half], bsend.at[step, half], brecv.at[x, half],
            lax.rem(r + 4 * step, rows), c,
        )

    @pl.when(core1)
    def _():
        to_pair.wait_recv()
        first = pair == 0

        @pl.when(pair == 1)
        def _():
            prefix.start()

        late_g = jnp.where(first, abuf[0], fbuf[0])
        late_b = jnp.where(first, abuf[1], fbuf[1])
        early_pair = jnp.where(first, both(fbuf), both(abuf))
        w = mm(late_g, early_pair)
        hbuf[0] = w[:, :nb]
        hbuf[1] = w[:, nb:] + late_b
        for step in range(groups - 1, 0, -1):
            @pl.when(x + step < groups)
            def _(step=step):
                along_x(step, 1).start()

                @pl.when(x > 0)
                def _():
                    along_x(step, 0).start()

    @pl.when(core1)
    def _():
        third.wait_recv()
        c4, d4 = done(1, g3[:, 0:part], g3[:, part : 2 * part])
        w = mm(c4, both(ebuf))
        cbuf[2 * nb : 3 * nb] = w[:, :nb]
        dbuf[2 * nb : 3 * nb] = w[:, nb:] + d4

    @pl.when(core1 & (pair == 0))
    def _():
        pbuf[...] = p1buf[...]

    @pl.when(core1 & (pair == 1))
    def _():
        w = mm(p1buf[0], both(abuf))
        pbuf[0] = w[:, :nb]
        pbuf[1] = w[:, nb:] + p1buf[1]

    @pl.when(core0 & (pair == 1))
    def _():
        prefix.wait_recv()

    @pl.when(core1 | (pair == 1))
    def _():
        w = mm(cbuf[...], both(pbuf))
        cbuf[...] = w[:, :nb]
        dbuf[...] = w[:, nb:] + dbuf[...]

    @pl.when(x == 0)
    def _():
        sbuf[...] = s0

    @pl.when((x > 0) & core1)
    def _():
        for source in range(groups - 1):
            @pl.when(x > source)
            def _(source=source):
                await_bytes(bbuf.at[source, 1], brecv.at[source, 1])
                if source:
                    await_bytes(bbuf.at[source, 0], brecv.at[source, 0])
                    sbuf[...] = mm(bbuf[source, 0], sbuf[...]) + bbuf[source, 1]
                else:
                    sbuf[...] = bbuf[source, 1]
        state.start()

    @pl.when((x > 0) & core0)
    def _():
        state.wait_recv()

    dbuf[...] = mm(cbuf[...], sbuf[...]) + dbuf[...]
    y_ref[...] = dbuf[pl.ds(nb - off, own)]

    await_bytes(got1, s1.at[0])
    head.wait_send()
    await_bytes(stage.at[pl.ds(0, chips - 1)], s2.at[0])

    @pl.when(core0)
    def _():
        await_bytes(stage.at[0], s2.at[0])
        tail.wait_send()

    @pl.when(core1)
    def _():
        entries.wait_send()
        third.wait_send()
        to_pair.wait_send()

        @pl.when(pair == 1)
        def _():
            prefix.wait_send()

        @pl.when(x > 0)
        def _():
            state.wait_send()

        for step in range(1, groups):
            @pl.when(x + step < groups)
            def _(step=step):
                along_x(step, 1).wait_send()

                @pl.when(x > 0)
                def _():
                    along_x(step, 0).wait_send()


def solution(mesh):
    rows, cols = mesh.shape["row"], mesh.shape["col"]

    def on_device(eigvecs, offsets, plan, refl_v, refl_t):
        own, width = eigvecs.shape
        nb = refl_t.shape[1]
        part = nb // rows
        dma = pltpu.SemaphoreType.DMA
        square = (nb, nb)
        y = pl.pallas_call(
            functools.partial(kernel, rows, cols),
            out_shape=pltpu.VMEM((own, width), F32),
            in_specs=[
                pl.BlockSpec(memory_space=pl.ANY),
                pl.BlockSpec(memory_space=pl.ANY),
                pl.BlockSpec(memory_space=pl.ANY),
                pl.BlockSpec(memory_space=pl.ANY),
                pl.BlockSpec(memory_space=pl.ANY),
            ],
            out_specs=pl.BlockSpec(memory_space=pltpu.VMEM),
            scratch_shapes=[
                pltpu.SMEM(offsets.shape, jnp.int32),
                pltpu.SMEM(plan.shape, jnp.int32),
                pltpu.VMEM((3 * own, width), F32),
                pltpu.VMEM((5, nb, width), F32),
                pltpu.VMEM((2, part, nb), F32),
                pltpu.VMEM((2, part, nb), F32),
                pltpu.VMEM((2, 2 * part, nb), F32),
                pltpu.VMEM((cols, 2 * part, nb), F32),
                pltpu.VMEM((rows // 2, 8 * part, nb), F32),
                pltpu.VMEM((rows, 8 * part, nb), F32),
                pltpu.VMEM((rows, 2 * part, nb), F32),
                pltpu.VMEM((2,) + square, F32),
                pltpu.VMEM((2,) + square, F32),
                pltpu.VMEM((2,) + square, F32),
                pltpu.VMEM((2,) + square, F32),
                pltpu.VMEM((2,) + square, F32),
                pltpu.VMEM((rows // 4, 2) + square, F32),
                pltpu.VMEM((2,) + square, F32),
                pltpu.VMEM(square, F32),
                pltpu.VMEM((3 * nb, nb), F32),
                pltpu.VMEM((3 * nb, width), F32),
                dma((3,)), dma((2, 4)), dma((4,)), dma((2,)), dma((2,)), dma((2,)), dma((2,)), dma((2,)), dma((2,)),
                dma((rows // 4, 2)), dma((rows // 4, 2)), dma((2,)),
                pltpu.SemaphoreType.REGULAR, pltpu.SemaphoreType.REGULAR,
                pltpu.SemaphoreType.REGULAR,
            ],
            compiler_params=pltpu.CompilerParams(
                collective_id=0, has_side_effects=True, vmem_limit_bytes=60 * 2**20
            ),
            cost_estimate=pl.CostEstimate(
                flops=2 * 30 * nb**3, bytes_accessed=4 * 10 * nb * nb, transcendentals=0
            ),
            name="chase",
        )(offsets, plan, eigvecs, refl_v.transpose(1, 0, 2), refl_t)
        return y

    return jax.shard_map(
        on_device,
        mesh=mesh,
        in_specs=(P("row", "col"), P(), P(), P("col", None, None), P("col", None, None)),
        out_specs=P("row", "col"),
        check_vma=False,
    )
```

```python
import functools

import jax
import jax.numpy as jnp
from jax import lax
from jax.experimental import pallas as pl
from jax.experimental.pallas import tpu as pltpu
from jax.sharding import PartitionSpec as P

MESH = pl.DeviceIdType.MESH
F32 = jnp.float32
BF16 = jnp.bfloat16


def split(a):
    hi = a.astype(BF16)
    return hi, (a - hi.astype(F32)).astype(BF16)


def mm(a, b, rhs_t=False):
    ah, al = split(a)
    bh, bl = split(b)
    dot = functools.partial(
        lax.dot_general,
        dimension_numbers=(((1,), (1 if rhs_t else 0,)), ((), ())),
        preferred_element_type=F32,
    )
    if rhs_t:
        return dot(ah, bl) + dot(al, bh) + dot(ah, bh)
    return dot(ah, bl) + dot(
        jnp.concatenate([ah, al], axis=1), jnp.concatenate([bh, bh], axis=0)
    )


def both(pair):
    return jnp.concatenate([pair[0], pair[1]], axis=1)


def classes(cols):
    if cols == 32:
        start_z = (0.0, 0.9, 1.9, 2.8, 5.8, 6.7, 7.6, 8.4)
        start_y = (0.4, 2.2, 4.7, 3.3)
        start = {4 * z + y: start_z[z] + start_y[y] for z in range(8) for y in range(4)}
        served = {(5, 0): (4, 0), (6, 0): (3, 0), (7, 0): (1, 0), (3, 2): (2, 2)}
        for y in (1, 2, 3):
            served.update({(4 + k, y): (3 - k, y) for k in range(4)})
        served[4, 2] = (2, 2)
        partner = {4 * a + b: 4 * d + e for (a, b), (d, e) in served.items()}
    else:
        start = {k: k for k in range(cols)}
        partner = {k: k - cols // 2 for k in range((cols + 1) // 2, cols)}
    order = sorted(start, key=lambda k: start[k])
    early = [k for k in order if k not in partner]
    return early, [k for k in order if k in partner], partner


def kernel(
    rows, cols, off_hbm, plan_hbm, e_ref, v_ref, t_ref, y_ref,
    off_ref, plan_ref, xin, xt, low, up, mine, g1, stage, g2, g3, ebuf, p1buf, fbuf, abuf, hbuf, bbuf, pbuf, sbuf, cbuf, dbuf,
    lsem, msem, hsem, s1, s2, s3, esem, psem, asem, bsend, brecv, dsem, rowsem, colsem, gosem,
):
    nb = t_ref.shape[1]
    part = nb // rows
    own = e_ref.shape[0]
    r = lax.axis_index("row")
    c = lax.axis_index("col")
    core, pair, x = r % 2, (r // 2) % 2, r // 4
    groups = rows // 4
    early, late, partner = classes(cols)
    blocks = 2 * rows - 2

    is_late = functools.reduce(jnp.logical_or, [c == k for k in late])
    server = sum(jnp.where(c == a, b, 0) for a, b in partner.items())
    is_early = jnp.logical_not(is_late)

    def row_at(k):
        return lax.rem(r + k, rows)

    swaps = cols % 8 == 0

    def across(k):
        return (lax.rem(c - k + 4 * cols, 4) == 2).astype(jnp.int32) if swaps else 0

    def row_for(k):
        return r ^ (2 * across(k))

    def remote(src, dst, send, recv, to_row, to_col):
        return pltpu.make_async_remote_copy(
            src_ref=src, dst_ref=dst, send_sem=send, recv_sem=recv,
            device_id=(to_row, to_col), device_id_type=MESH,
        )

    def signal(sem, to_row, to_col):
        pl.semaphore_signal(sem, 1, device_id=(to_row, to_col), device_id_type=MESH)

    def await_bytes(ref, sem):
        pltpu.make_async_copy(ref, ref, sem).wait()

    mine_parts = []
    for i in range(1 + swaps):
        at = pl.multiple_of((r ^ (2 * i)) * part, part)
        end = jnp.minimum(nb + at + part - 1, 2 * nb - 2)
        mine_parts += [
            pltpu.make_async_copy(v_ref.at[pl.ds(at, part), 0], low.at[i], msem.at[i, 0]),
            pltpu.make_async_copy(
                v_ref.at[pl.ds(nb + at, part - 1), 0],
                up.at[i, pl.ds(0, part - 1)],
                msem.at[i, 1],
            ),
            pltpu.make_async_copy(
                v_ref.at[pl.ds(end, 1), 0], up.at[i, pl.ds(part - 1, 1)], msem.at[i, 2]
            ),
            pltpu.make_async_copy(
                t_ref.at[0, pl.ds(at, part)], mine.at[i, pl.ds(part, part)], msem.at[i, 3]
            ),
        ]
    get_e = pltpu.make_async_copy(e_ref, xin.at[pl.ds(own, own)], lsem.at[0])
    get_plan = pltpu.make_async_copy(plan_hbm, plan_ref, lsem.at[1])
    get_off = pltpu.make_async_copy(off_hbm, off_ref, lsem.at[2])
    for copy in mine_parts:
        copy.start()

    barrier = pltpu.get_barrier_semaphore()

    @pl.when(is_early)
    def _():
        for k in late[::-1] + early[::-1]:
            @pl.when(c != k)
            def _(k=k):
                signal(barrier, row_for(k), k)
        for k in range(1, rows):
            signal(barrier, row_at(k), c)

        for a, b in partner.items():
            @pl.when(c == b)
            def _(a=a):
                for k in range(1, rows):
                    signal(barrier, row_at(k), a)

    @pl.when(is_late)
    def _():
        pl.semaphore_wait(barrier, len(early) + rows - 1)
        for k in early:
            signal(colsem, row_for(k), k)
        for k in range(1, rows):
            signal(rowsem, row_at(k), server)

    @pl.when(core == 0)
    def _():
        xin[own - nb : own] = jnp.zeros((nb, nb), F32)

    for copy in mine_parts:
        copy.wait()
    for i in range(1 + swaps):
        at = (r ^ (2 * i)) * part
        row_ids = lax.broadcasted_iota(jnp.int32, (part, nb), 0) + at
        col_ids = lax.broadcasted_iota(jnp.int32, (part, nb), 1)
        mine[i, 0:part] = jnp.where(row_ids >= col_ids, low[i], up[i])

    @pl.when(is_early)
    def _():
        pl.semaphore_wait(barrier, len(early) - 1 + rows - 1)

    def share(to):
        for k in to:
            @pl.when(c != k)
            def _(k=k):
                remote(
                    mine.at[across(k)], g1.at[c], s1.at[0], s1.at[1], row_for(k), k
                ).start()

    share(early)
    for copy in (get_e, get_plan, get_off):
        copy.start()
    head = remote(
        e_ref, xin.at[pl.ds(2 * own, own)], hsem.at[0], hsem.at[1], row_at(rows - 1), c
    )
    tail = remote(e_ref, xin.at[pl.ds(0, own)], hsem.at[2], hsem.at[3], r ^ 1, c)

    def send_rows():
        head.start()

        @pl.when(core == 0)
        def _():
            tail.start()

    got1 = g1.at[pl.ds(0, cols - 1)]
    g1[c] = mine[0]

    @pl.when(is_early)
    def _():
        send_rows()
        pl.semaphore_wait(colsem, len(late))
        for b in sorted(set(partner.values())):
            served = [k for k in late if partner[k] == b]

            @pl.when(c == b)
            def _(served=served):
                pl.semaphore_wait(rowsem, (rows - 1) * len(served))
                for a in served:
                    signal(gosem, r, a)

        share(late)

    @pl.when(is_late)
    def _():
        pl.semaphore_wait(gosem, 1)
        share(late)
        send_rows()

    await_bytes(got1, s1.at[1])
    get_plan.wait()
    get_off.wait()

    chips = rows // 2
    chip = r // 2
    core0, core1 = core == 0, core == 1
    order = sorted(range(1, chips), key=lambda k: -min(k, chips - k)) + [0]

    def wave(h):
        return pl.ds(4 * part * h, 4 * part)

    def to_chip(k, h):
        to = 2 * lax.rem(chip + k, chips) + 1
        return remote(
            stage.at[k, wave(h)], g2.at[r, wave(h)], s2.at[0, h], s2.at[1, h], to, c
        )

    for h in range(2):
        for k in order:
            for j in (2 * h, 2 * h + 1):
                block = jnp.clip(4 * lax.rem(chip + k, chips) - 1 + j, 0, blocks - 1)
                stage[k, 2 * part * j : 2 * part * (j + 1)] = g1[plan_ref[0, block]]
        for k in order[:-1]:
            to_chip(k, h).start()

        @pl.when(core0)
        def _(h=h):
            to_chip(0, h).start()

    @pl.when(core1)
    def _():
        g2[r] = stage[0]
        tail.wait_recv()

    get_e.wait()
    head.wait_recv()
    off = off_ref[0]
    s0 = xin[pl.ds(off + own - nb, nb)]

    ri = lax.broadcasted_iota(jnp.int32, (nb, nb), 0)
    ci = lax.broadcasted_iota(jnp.int32, (nb, nb), 1)
    eye = (ri == ci).astype(F32)

    def triangles(packed):
        packed = packed.reshape(nb, nb)
        return jnp.where(ri >= ci, packed, 0.0), jnp.where(ri >= ci, 0.0, packed)

    def fresh(n):
        return xin[pl.ds(off + own + nb * (n + 1), nb)]

    def entry(j):
        lo = 2 * part * j
        return g2[:, lo : lo + part], g2[:, lo + part : lo + 2 * part]

    def keep_transposed(blocks_of):
        for n in blocks_of:
            xt[n + 3] = fresh(n).T

    def live(n, factor):
        inside = ((2 * r + n >= 0) & (2 * r + n < blocks)).astype(F32)
        return factor.reshape(nb, nb) * inside

    def sides(n, lower, upper):
        return jnp.concatenate([lower, mm(xt[n + 3], upper)], axis=0)

    def passed(n, packed, factor):
        lower, upper = triangles(packed)
        w = mm(mm(upper, live(n, factor)), sides(n, lower, upper), rhs_t=True)
        return -w[:, :nb], fresh(n) - w[:, nb:]

    def done(n, packed, factor):
        lower, upper = triangles(packed)
        w = mm(mm(lower, live(n, factor)), sides(n, lower, upper), rhs_t=True)
        return eye - w[:, :nb], -w[:, nb:]

    entries = remote(
        g2.at[:, pl.ds(0, 6 * part)], g2.at[:, pl.ds(0, 6 * part)],
        esem.at[0], esem.at[1], r ^ 1, c,
    )
    third = remote(
        g2.at[:, pl.ds(0, 2 * part)], g3, s3.at[0], s3.at[1], row_at(rows - 2), c
    )
    to_pair = remote(fbuf, abuf, asem.at[0], asem.at[1], r ^ 2, c)
    prefix = remote(abuf, pbuf, psem.at[0], psem.at[1], r ^ 1, c)
    state = remote(sbuf, sbuf, dsem.at[0], dsem.at[1], r ^ 1, c)

    @pl.when(core1)
    def _():
        keep_transposed(range(-3, 2))
        await_bytes(g2.at[pl.ds(0, rows - 1), wave(0)], s2.at[1, 0])
        third.start()
        (a0, b0), (a1, b1) = [passed(j - 3, *entry(j)) for j in (0, 1)]
        first = mm(a1, jnp.concatenate([a0, b0], axis=1))
        p1buf[0] = first[:, :nb]
        p1buf[1] = first[:, nb:] + b1
        await_bytes(g2.at[pl.ds(0, rows - 1), wave(1)], s2.at[1, 1])
        (a2, b2), (a3, b3) = [passed(j - 3, *entry(j)) for j in (2, 3)]
        second = mm(a3, jnp.concatenate([a2, b2], axis=1))
        ebuf[0] = second[:, :nb]
        ebuf[1] = second[:, nb:] + b3
        w = mm(ebuf[0], both(p1buf))
        fbuf[0] = w[:, :nb]
        fbuf[1] = w[:, nb:] + ebuf[1]
        to_pair.start()
        entries.start()
        c2, d2 = done(-1, *entry(2))
        cbuf[0:nb] = c2
        dbuf[0:nb] = d2
        c3, d3 = done(0, *entry(3))
        w = mm(c3, jnp.concatenate([a2, b2], axis=1))
        cbuf[nb : 2 * nb] = w[:, :nb]
        dbuf[nb : 2 * nb] = w[:, nb:] + d3

    @pl.when(core0)
    def _():
        keep_transposed(range(-1, 2))
        await_bytes(g2.at[:, pl.ds(0, 6 * part)], esem.at[1])
        (a0, b0), (a1, b1) = [passed(j - 1, *entry(j)) for j in range(2)]
        (c0, d0), (c1, d1), (c2, d2) = [done(j - 1, *entry(j)) for j in range(3)]
        cbuf[0:nb] = c0
        dbuf[0:nb] = d0
        w = mm(jnp.concatenate([a1, c1], axis=0), jnp.concatenate([a0, b0], axis=1))
        cbuf[nb : 2 * nb] = w[nb:, :nb]
        dbuf[nb : 2 * nb] = w[nb:, nb:] + d1
        g, b = w[:nb, :nb], w[:nb, nb:] + b1
        w = mm(c2, jnp.concatenate([g, b], axis=1))
        cbuf[2 * nb : 3 * nb] = w[:, :nb]
        dbuf[2 * nb : 3 * nb] = w[:, nb:] + d2

    def along_x(step, half):
        return remote(
            hbuf.at[half], bbuf.at[x, half], bsend.at[step, half], brecv.at[x, half],
            lax.rem(r + 4 * step, rows), c,
        )

    @pl.when(core1)
    def _():
        to_pair.wait_recv()
        first = pair == 0

        @pl.when(pair == 1)
        def _():
            prefix.start()

        late_g = jnp.where(first, abuf[0], fbuf[0])
        late_b = jnp.where(first, abuf[1], fbuf[1])
        early_pair = jnp.where(first, both(fbuf), both(abuf))
        w = mm(late_g, early_pair)
        hbuf[0] = w[:, :nb]
        hbuf[1] = w[:, nb:] + late_b
        for step in range(groups - 1, 0, -1):
            @pl.when(x + step < groups)
            def _(step=step):
                along_x(step, 1).start()

                @pl.when(x > 0)
                def _():
                    along_x(step, 0).start()

    @pl.when(core1)
    def _():
        third.wait_recv()
        c4, d4 = done(1, g3[:, 0:part], g3[:, part : 2 * part])
        w = mm(c4, both(ebuf))
        cbuf[2 * nb : 3 * nb] = w[:, :nb]
        dbuf[2 * nb : 3 * nb] = w[:, nb:] + d4

    @pl.when(core1 & (pair == 0))
    def _():
        pbuf[...] = p1buf[...]

    @pl.when(core1 & (pair == 1))
    def _():
        w = mm(p1buf[0], both(abuf))
        pbuf[0] = w[:, :nb]
        pbuf[1] = w[:, nb:] + p1buf[1]

    @pl.when(core0 & (pair == 1))
    def _():
        prefix.wait_recv()

    @pl.when(core1 | (pair == 1))
    def _():
        w = mm(cbuf[...], both(pbuf))
        cbuf[...] = w[:, :nb]
        dbuf[...] = w[:, nb:] + dbuf[...]

    @pl.when(x == 0)
    def _():
        sbuf[...] = s0

    @pl.when((x > 0) & core1)
    def _():
        for source in range(groups - 1):
            @pl.when(x > source)
            def _(source=source):
                await_bytes(bbuf.at[source, 1], brecv.at[source, 1])
                if source:
                    await_bytes(bbuf.at[source, 0], brecv.at[source, 0])
                    sbuf[...] = mm(bbuf[source, 0], sbuf[...]) + bbuf[source, 1]
                else:
                    sbuf[...] = bbuf[source, 1]
        state.start()

    @pl.when((x > 0) & core0)
    def _():
        state.wait_recv()

    dbuf[...] = mm(cbuf[...], sbuf[...]) + dbuf[...]
    y_ref[...] = dbuf[pl.ds(nb - off, own)]

    await_bytes(got1, s1.at[0])
    head.wait_send()
    for h in range(2):
        await_bytes(stage.at[pl.ds(0, chips - 1), wave(h)], s2.at[0, h])

    @pl.when(core0)
    def _():
        for h in range(2):
            await_bytes(stage.at[0, wave(h)], s2.at[0, h])
        tail.wait_send()

    @pl.when(core1)
    def _():
        entries.wait_send()
        third.wait_send()
        to_pair.wait_send()

        @pl.when(pair == 1)
        def _():
            prefix.wait_send()

        @pl.when(x > 0)
        def _():
            state.wait_send()

        for step in range(1, groups):
            @pl.when(x + step < groups)
            def _(step=step):
                along_x(step, 1).wait_send()

                @pl.when(x > 0)
                def _():
                    along_x(step, 0).wait_send()


def solution(mesh):
    rows, cols = mesh.shape["row"], mesh.shape["col"]

    def on_device(eigvecs, offsets, plan, refl_v, refl_t):
        own, width = eigvecs.shape
        nb = refl_t.shape[1]
        part = nb // rows
        dma = pltpu.SemaphoreType.DMA
        square = (nb, nb)
        y = pl.pallas_call(
            functools.partial(kernel, rows, cols),
            out_shape=pltpu.VMEM((own, width), F32),
            in_specs=[
                pl.BlockSpec(memory_space=pl.ANY),
                pl.BlockSpec(memory_space=pl.ANY),
                pl.BlockSpec(memory_space=pl.ANY),
                pl.BlockSpec(memory_space=pl.ANY),
                pl.BlockSpec(memory_space=pl.ANY),
            ],
            out_specs=pl.BlockSpec(memory_space=pltpu.VMEM),
            scratch_shapes=[
                pltpu.SMEM(offsets.shape, jnp.int32),
                pltpu.SMEM(plan.shape, jnp.int32),
                pltpu.VMEM((3 * own, width), F32),
                pltpu.VMEM((5, nb, width), F32),
                pltpu.VMEM((2, part, nb), F32),
                pltpu.VMEM((2, part, nb), F32),
                pltpu.VMEM((2, 2 * part, nb), F32),
                pltpu.VMEM((cols, 2 * part, nb), F32),
                pltpu.VMEM((rows // 2, 8 * part, nb), F32),
                pltpu.VMEM((rows, 8 * part, nb), F32),
                pltpu.VMEM((rows, 2 * part, nb), F32),
                pltpu.VMEM((2,) + square, F32),
                pltpu.VMEM((2,) + square, F32),
                pltpu.VMEM((2,) + square, F32),
                pltpu.VMEM((2,) + square, F32),
                pltpu.VMEM((2,) + square, F32),
                pltpu.VMEM((rows // 4, 2) + square, F32),
                pltpu.VMEM((2,) + square, F32),
                pltpu.VMEM(square, F32),
                pltpu.VMEM((3 * nb, nb), F32),
                pltpu.VMEM((3 * nb, width), F32),
                dma((3,)), dma((2, 4)), dma((4,)), dma((2,)), dma((2, 2)), dma((2,)), dma((2,)), dma((2,)), dma((2,)),
                dma((rows // 4, 2)), dma((rows // 4, 2)), dma((2,)),
                pltpu.SemaphoreType.REGULAR, pltpu.SemaphoreType.REGULAR,
                pltpu.SemaphoreType.REGULAR,
            ],
            compiler_params=pltpu.CompilerParams(
                collective_id=0, has_side_effects=True, vmem_limit_bytes=60 * 2**20
            ),
            cost_estimate=pl.CostEstimate(
                flops=2 * 30 * nb**3, bytes_accessed=4 * 10 * nb * nb, transcendentals=0
            ),
            name="chase",
        )(offsets, plan, eigvecs, refl_v.transpose(1, 0, 2), refl_t)
        return y

    return jax.shard_map(
        on_device,
        mesh=mesh,
        in_specs=(P("row", "col"), P(), P(), P("col", None, None), P("col", None, None)),
        out_specs=P("row", "col"),
        check_vma=False,
    )
```

```python
import functools

import jax
import jax.numpy as jnp
from jax import lax
from jax.experimental import pallas as pl
from jax.experimental.pallas import tpu as pltpu
from jax.sharding import PartitionSpec as P

MESH = pl.DeviceIdType.MESH
F32 = jnp.float32
BF16 = jnp.bfloat16


def split(a):
    hi = a.astype(BF16)
    return hi, (a - hi.astype(F32)).astype(BF16)


def mm(a, b, rhs_t=False):
    ah, al = split(a)
    bh, bl = split(b)
    dot = functools.partial(
        lax.dot_general,
        dimension_numbers=(((1,), (1 if rhs_t else 0,)), ((), ())),
        preferred_element_type=F32,
    )
    if rhs_t:
        return dot(ah, bl) + dot(al, bh) + dot(ah, bh)
    return dot(ah, bl) + dot(
        jnp.concatenate([ah, al], axis=1), jnp.concatenate([bh, bh], axis=0)
    )


def both(pair):
    return jnp.concatenate([pair[0], pair[1]], axis=1)


def classes(cols):
    if cols == 32:
        start_z = (0.0, 0.9, 1.9, 2.8, 5.8, 6.7, 7.6, 8.4)
        start_y = (0.4, 2.2, 4.7, 3.3)
        start = {4 * z + y: start_z[z] + start_y[y] for z in range(8) for y in range(4)}
        served = {(5, 0): (4, 0), (6, 0): (3, 0), (7, 0): (1, 0), (3, 2): (2, 2)}
        for y in (1, 2, 3):
            served.update({(4 + k, y): (3 - k, y) for k in range(4)})
        served[4, 2] = (2, 2)
        partner = {4 * a + b: 4 * d + e for (a, b), (d, e) in served.items()}
    else:
        start = {k: k for k in range(cols)}
        partner = {k: k - cols // 2 for k in range((cols + 1) // 2, cols)}
    order = sorted(start, key=lambda k: start[k])
    early = [k for k in order if k not in partner]
    return early, [k for k in order if k in partner], partner


def kernel(
    rows, cols, off_hbm, plan_hbm, e_ref, v_ref, t_ref, y_ref,
    off_ref, plan_ref, xin, xt, low, up, mine, g1, stage, g2, g3, ebuf, p1buf, fbuf, abuf, hbuf, bbuf, pbuf, sbuf, cbuf, dbuf,
    lsem, msem, hsem, s1, s2, s3, esem, psem, asem, bsend, brecv, dsem, rowsem, colsem, gosem,
):
    nb = t_ref.shape[1]
    part = nb // rows
    own = e_ref.shape[0]
    r = lax.axis_index("row")
    c = lax.axis_index("col")
    core, pair, x = r % 2, (r // 2) % 2, r // 4
    groups = rows // 4
    early, late, partner = classes(cols)
    blocks = 2 * rows - 2

    is_late = functools.reduce(jnp.logical_or, [c == k for k in late])
    server = sum(jnp.where(c == a, b, 0) for a, b in partner.items())
    is_early = jnp.logical_not(is_late)

    def row_at(k):
        return lax.rem(r + k, rows)

    swaps = cols % 8 == 0

    def across(k):
        return (lax.rem(c - k + 4 * cols, 4) == 2).astype(jnp.int32) if swaps else 0

    def row_for(k):
        return r ^ (2 * across(k))

    def remote(src, dst, send, recv, to_row, to_col):
        return pltpu.make_async_remote_copy(
            src_ref=src, dst_ref=dst, send_sem=send, recv_sem=recv,
            device_id=(to_row, to_col), device_id_type=MESH,
        )

    def signal(sem, to_row, to_col):
        pl.semaphore_signal(sem, 1, device_id=(to_row, to_col), device_id_type=MESH)

    def await_bytes(ref, sem):
        pltpu.make_async_copy(ref, ref, sem).wait()

    mine_parts = []
    for i in range(1 + swaps):
        at = pl.multiple_of((r ^ (2 * i)) * part, part)
        end = jnp.minimum(nb + at + part - 1, 2 * nb - 2)
        mine_parts += [
            pltpu.make_async_copy(v_ref.at[pl.ds(at, part), 0], low.at[i], msem.at[i, 0]),
            pltpu.make_async_copy(
                v_ref.at[pl.ds(nb + at, part - 1), 0],
                up.at[i, pl.ds(0, part - 1)],
                msem.at[i, 1],
            ),
            pltpu.make_async_copy(
                v_ref.at[pl.ds(end, 1), 0], up.at[i, pl.ds(part - 1, 1)], msem.at[i, 2]
            ),
            pltpu.make_async_copy(
                t_ref.at[0, pl.ds(at, part)], mine.at[i, pl.ds(part, part)], msem.at[i, 3]
            ),
        ]
    get_e = pltpu.make_async_copy(e_ref, xin.at[pl.ds(own, own)], lsem.at[0])
    get_plan = pltpu.make_async_copy(plan_hbm, plan_ref, lsem.at[1])
    get_off = pltpu.make_async_copy(off_hbm, off_ref, lsem.at[2])
    for copy in mine_parts:
        copy.start()

    barrier = pltpu.get_barrier_semaphore()

    @pl.when(is_early)
    def _():
        for k in late[::-1] + early[::-1]:
            @pl.when(c != k)
            def _(k=k):
                signal(barrier, row_for(k), k)
        for k in range(1, rows):
            signal(barrier, row_at(k), c)

        for a, b in partner.items():
            @pl.when(c == b)
            def _(a=a):
                for k in range(1, rows):
                    signal(barrier, row_at(k), a)

    @pl.when(is_late)
    def _():
        pl.semaphore_wait(barrier, len(early) + rows - 1)
        for k in early:
            signal(colsem, row_for(k), k)
        for k in range(1, rows):
            signal(rowsem, row_at(k), server)

    @pl.when(core == 0)
    def _():
        xin[own - nb : own] = jnp.zeros((nb, nb), F32)

    for copy in mine_parts:
        copy.wait()
    for i in range(1 + swaps):
        at = (r ^ (2 * i)) * part
        row_ids = lax.broadcasted_iota(jnp.int32, (part, nb), 0) + at
        col_ids = lax.broadcasted_iota(jnp.int32, (part, nb), 1)
        mine[i, 0:part] = jnp.where(row_ids >= col_ids, low[i], up[i])

    @pl.when(is_early)
    def _():
        pl.semaphore_wait(barrier, len(early) - 1 + rows - 1)

    def share(to):
        for k in to:
            @pl.when(c != k)
            def _(k=k):
                remote(
                    mine.at[across(k)], g1.at[c], s1.at[0], s1.at[1], row_for(k), k
                ).start()

    share(early)
    for copy in (get_e, get_plan, get_off):
        copy.start()
    head = remote(
        e_ref, xin.at[pl.ds(2 * own, own)], hsem.at[0], hsem.at[1], row_at(rows - 1), c
    )
    tail = remote(e_ref, xin.at[pl.ds(0, own)], hsem.at[2], hsem.at[3], r ^ 1, c)

    def send_rows():
        head.start()

        @pl.when(core == 0)
        def _():
            tail.start()

    got1 = g1.at[pl.ds(0, cols - 1)]
    g1[c] = mine[0]

    @pl.when(is_early)
    def _():
        send_rows()
        pl.semaphore_wait(colsem, len(late))
        for b in sorted(set(partner.values())):
            served = [k for k in late if partner[k] == b]

            @pl.when(c == b)
            def _(served=served):
                pl.semaphore_wait(rowsem, (rows - 1) * len(served))
                for a in served:
                    signal(gosem, r, a)

        share(late)

    @pl.when(is_late)
    def _():
        pl.semaphore_wait(gosem, 1)
        share(late)
        send_rows()

    await_bytes(got1, s1.at[1])
    get_plan.wait()
    get_off.wait()

    chips = rows // 2
    chip = r // 2
    core0, core1 = core == 0, core == 1
    order = sorted(range(1, chips), key=lambda k: -min(k, chips - k)) + [0]

    def wave(h):
        return pl.ds(4 * part * h, 4 * part)

    def to_chip(k, h):
        to = 2 * lax.rem(chip + k, chips) + 1
        return remote(
            stage.at[k, wave(h)], g2.at[r, wave(h)], s2.at[0, h], s2.at[1, h], to, c
        )

    for h in range(2):
        for k in order:
            for j in (2 * h, 2 * h + 1):
                block = jnp.clip(4 * lax.rem(chip + k, chips) - 1 + j, 0, blocks - 1)
                stage[k, 2 * part * j : 2 * part * (j + 1)] = g1[plan_ref[0, block]]
        for k in order[:-1]:
            to_chip(k, h).start()

        @pl.when(core0)
        def _(h=h):
            to_chip(0, h).start()

    @pl.when(core1)
    def _():
        g2[r] = stage[0]
        tail.wait_recv()

    get_e.wait()
    head.wait_recv()
    off = off_ref[0]
    s0 = xin[pl.ds(off + own - nb, nb)]

    ri = lax.broadcasted_iota(jnp.int32, (nb, nb), 0)
    ci = lax.broadcasted_iota(jnp.int32, (nb, nb), 1)
    eye = (ri == ci).astype(F32)

    def triangles(packed):
        packed = packed.reshape(nb, nb)
        return jnp.where(ri >= ci, packed, 0.0), jnp.where(ri >= ci, 0.0, packed)

    def fresh(n):
        return xin[pl.ds(off + own + nb * (n + 1), nb)]

    def entry(j):
        lo = 2 * part * j
        return g2[:, lo : lo + part], g2[:, lo + part : lo + 2 * part]

    def keep_transposed(blocks_of):
        for n in blocks_of:
            xt[n + 3] = fresh(n).T

    def live(n, factor):
        inside = ((2 * r + n >= 0) & (2 * r + n < blocks)).astype(F32)
        return factor.reshape(nb, nb) * inside

    def sides(n, lower, upper):
        return jnp.concatenate([lower, mm(xt[n + 3], upper)], axis=0)

    def passed(n, packed, factor):
        lower, upper = triangles(packed)
        w = mm(mm(upper, live(n, factor)), sides(n, lower, upper), rhs_t=True)
        return -w[:, :nb], fresh(n) - w[:, nb:]

    def done(n, packed, factor):
        lower, upper = triangles(packed)
        w = mm(mm(lower, live(n, factor)), sides(n, lower, upper), rhs_t=True)
        return eye - w[:, :nb], -w[:, nb:]

    entries = remote(
        g2.at[:, pl.ds(0, 6 * part)], g2.at[:, pl.ds(0, 6 * part)],
        esem.at[0], esem.at[1], r ^ 1, c,
    )
    third = remote(
        g2.at[:, pl.ds(0, 2 * part)], g3, s3.at[0], s3.at[1], row_at(rows - 2), c
    )
    to_pair = remote(fbuf, abuf, asem.at[0], asem.at[1], r ^ 2, c)
    prefix = remote(abuf, pbuf, psem.at[0], psem.at[1], r ^ 1, c)
    state = remote(sbuf, sbuf, dsem.at[0], dsem.at[1], r ^ 1, c)

    @pl.when(core1)
    def _():
        keep_transposed(range(-3, 2))
        await_bytes(g2.at[pl.ds(0, rows - 1), wave(0)], s2.at[1, 0])
        third.start()
        (a0, b0), (a1, b1) = [passed(j - 3, *entry(j)) for j in (0, 1)]
        first = mm(a1, jnp.concatenate([a0, b0], axis=1))
        p1buf[0] = first[:, :nb]
        p1buf[1] = first[:, nb:] + b1
        await_bytes(g2.at[pl.ds(0, rows - 1), wave(1)], s2.at[1, 1])
        (a2, b2), (a3, b3) = [passed(j - 3, *entry(j)) for j in (2, 3)]
        second = mm(a3, jnp.concatenate([a2, b2], axis=1))
        ebuf[0] = second[:, :nb]
        ebuf[1] = second[:, nb:] + b3
        w = mm(ebuf[0], both(p1buf))
        fbuf[0] = w[:, :nb]
        fbuf[1] = w[:, nb:] + ebuf[1]
        to_pair.start()
        entries.start()
        c2, d2 = done(-1, *entry(2))
        cbuf[0:nb] = c2
        dbuf[0:nb] = d2
        c3, d3 = done(0, *entry(3))
        w = mm(c3, jnp.concatenate([a2, b2], axis=1))
        cbuf[nb : 2 * nb] = w[:, :nb]
        dbuf[nb : 2 * nb] = w[:, nb:] + d3

    @pl.when(core0)
    def _():
        keep_transposed(range(-1, 2))
        await_bytes(g2.at[:, pl.ds(0, 6 * part)], esem.at[1])
        (a0, b0), (a1, b1) = [passed(j - 1, *entry(j)) for j in range(2)]
        (c0, d0), (c1, d1), (c2, d2) = [done(j - 1, *entry(j)) for j in range(3)]
        cbuf[0:nb] = c0
        dbuf[0:nb] = d0
        w = mm(jnp.concatenate([a1, c1], axis=0), jnp.concatenate([a0, b0], axis=1))
        cbuf[nb : 2 * nb] = w[nb:, :nb]
        dbuf[nb : 2 * nb] = w[nb:, nb:] + d1
        g, b = w[:nb, :nb], w[:nb, nb:] + b1
        w = mm(c2, jnp.concatenate([g, b], axis=1))
        cbuf[2 * nb : 3 * nb] = w[:, :nb]
        dbuf[2 * nb : 3 * nb] = w[:, nb:] + d2

    def along_x(step, half):
        return remote(
            hbuf.at[half], bbuf.at[x, half], bsend.at[step, half], brecv.at[x, half],
            lax.rem(r + 4 * step, rows), c,
        )

    @pl.when(core1)
    def _():
        to_pair.wait_recv()
        first = pair == 0

        @pl.when(pair == 1)
        def _():
            prefix.start()

        late_g = jnp.where(first, abuf[0], fbuf[0])
        late_b = jnp.where(first, abuf[1], fbuf[1])
        early_pair = jnp.where(first, both(fbuf), both(abuf))
        w = mm(late_g, early_pair)
        hbuf[0] = w[:, :nb]
        hbuf[1] = w[:, nb:] + late_b
        for step in range(groups - 1, 0, -1):
            @pl.when(x + step < groups)
            def _(step=step):
                along_x(step, 1).start()

                @pl.when(x > 0)
                def _():
                    along_x(step, 0).start()

    @pl.when(core1)
    def _():
        third.wait_recv()
        c4, d4 = done(1, g3[:, 0:part], g3[:, part : 2 * part])
        w = mm(c4, both(ebuf))
        cbuf[2 * nb : 3 * nb] = w[:, :nb]
        dbuf[2 * nb : 3 * nb] = w[:, nb:] + d4

    @pl.when(core1 & (pair == 0))
    def _():
        pbuf[...] = p1buf[...]

    @pl.when(core1 & (pair == 1))
    def _():
        w = mm(p1buf[0], both(abuf))
        pbuf[0] = w[:, :nb]
        pbuf[1] = w[:, nb:] + p1buf[1]

    @pl.when(core0 & (pair == 1))
    def _():
        prefix.wait_recv()

    @pl.when(core1 | (pair == 1))
    def _():
        w = mm(cbuf[...], both(pbuf))
        cbuf[...] = w[:, :nb]
        dbuf[...] = w[:, nb:] + dbuf[...]

    gain = cbuf[pl.ds(nb - off, own)]
    rest = dbuf[pl.ds(nb - off, own)]

    await_bytes(got1, s1.at[0])
    head.wait_send()
    for h in range(2):
        await_bytes(stage.at[pl.ds(0, chips - 1), wave(h)], s2.at[0, h])

    @pl.when(core0)
    def _():
        for h in range(2):
            await_bytes(stage.at[0, wave(h)], s2.at[0, h])
        tail.wait_send()

    @pl.when(core1)
    def _():
        entries.wait_send()
        third.wait_send()
        to_pair.wait_send()

        @pl.when(pair == 1)
        def _():
            prefix.wait_send()

    @pl.when(x == 0)
    def _():
        sbuf[...] = s0

    @pl.when((x > 0) & core1)
    def _():
        for source in range(groups - 1):
            @pl.when(x > source)
            def _(source=source):
                await_bytes(bbuf.at[source, 1], brecv.at[source, 1])
                if source:
                    await_bytes(bbuf.at[source, 0], brecv.at[source, 0])
                    sbuf[...] = mm(bbuf[source, 0], sbuf[...]) + bbuf[source, 1]
                else:
                    sbuf[...] = bbuf[source, 1]
        state.start()

    @pl.when((x > 0) & core0)
    def _():
        state.wait_recv()

    y_ref[...] = mm(gain, sbuf[...]) + rest

    @pl.when((x > 0) & core1)
    def _():
        state.wait_send()

    @pl.when(core1)
    def _():
        for step in range(1, groups):
            @pl.when(x + step < groups)
            def _(step=step):
                along_x(step, 1).wait_send()

                @pl.when(x > 0)
                def _():
                    along_x(step, 0).wait_send()


def solution(mesh):
    rows, cols = mesh.shape["row"], mesh.shape["col"]

    def on_device(eigvecs, offsets, plan, refl_v, refl_t):
        own, width = eigvecs.shape
        nb = refl_t.shape[1]
        part = nb // rows
        dma = pltpu.SemaphoreType.DMA
        square = (nb, nb)
        y = pl.pallas_call(
            functools.partial(kernel, rows, cols),
            out_shape=pltpu.VMEM((own, width), F32),
            in_specs=[
                pl.BlockSpec(memory_space=pl.ANY),
                pl.BlockSpec(memory_space=pl.ANY),
                pl.BlockSpec(memory_space=pl.ANY),
                pl.BlockSpec(memory_space=pl.ANY),
                pl.BlockSpec(memory_space=pl.ANY),
            ],
            out_specs=pl.BlockSpec(memory_space=pltpu.VMEM),
            scratch_shapes=[
                pltpu.SMEM(offsets.shape, jnp.int32),
                pltpu.SMEM(plan.shape, jnp.int32),
                pltpu.VMEM((3 * own, width), F32),
                pltpu.VMEM((5, nb, width), F32),
                pltpu.VMEM((2, part, nb), F32),
                pltpu.VMEM((2, part, nb), F32),
                pltpu.VMEM((2, 2 * part, nb), F32),
                pltpu.VMEM((cols, 2 * part, nb), F32),
                pltpu.VMEM((rows // 2, 8 * part, nb), F32),
                pltpu.VMEM((rows, 8 * part, nb), F32),
                pltpu.VMEM((rows, 2 * part, nb), F32),
                pltpu.VMEM((2,) + square, F32),
                pltpu.VMEM((2,) + square, F32),
                pltpu.VMEM((2,) + square, F32),
                pltpu.VMEM((2,) + square, F32),
                pltpu.VMEM((2,) + square, F32),
                pltpu.VMEM((rows // 4, 2) + square, F32),
                pltpu.VMEM((2,) + square, F32),
                pltpu.VMEM(square, F32),
                pltpu.VMEM((3 * nb, nb), F32),
                pltpu.VMEM((3 * nb, width), F32),
                dma((3,)), dma((2, 4)), dma((4,)), dma((2,)), dma((2, 2)), dma((2,)), dma((2,)), dma((2,)), dma((2,)),
                dma((rows // 4, 2)), dma((rows // 4, 2)), dma((2,)),
                pltpu.SemaphoreType.REGULAR, pltpu.SemaphoreType.REGULAR,
                pltpu.SemaphoreType.REGULAR,
            ],
            compiler_params=pltpu.CompilerParams(
                collective_id=0, has_side_effects=True, vmem_limit_bytes=60 * 2**20
            ),
            cost_estimate=pl.CostEstimate(
                flops=2 * 30 * nb**3, bytes_accessed=4 * 10 * nb * nb, transcendentals=0
            ),
            name="chase",
        )(offsets, plan, eigvecs, refl_v.transpose(1, 0, 2), refl_t)
        return y

    return jax.shard_map(
        on_device,
        mesh=mesh,
        in_specs=(P("row", "col"), P(), P(), P("col", None, None), P("col", None, None)),
        out_specs=P("row", "col"),
        check_vma=False,
    )
```

```python
import functools

import jax
import jax.numpy as jnp
from jax import lax
from jax.experimental import pallas as pl
from jax.experimental.pallas import tpu as pltpu
from jax.sharding import PartitionSpec as P

MESH = pl.DeviceIdType.MESH
F32 = jnp.float32
BF16 = jnp.bfloat16


def split(a):
    hi = a.astype(BF16)
    return hi, (a - hi.astype(F32)).astype(BF16)


def mm(a, b, rhs_t=False):
    ah, al = split(a)
    bh, bl = split(b)
    dot = functools.partial(
        lax.dot_general,
        dimension_numbers=(((1,), (1 if rhs_t else 0,)), ((), ())),
        preferred_element_type=F32,
    )
    if rhs_t:
        return dot(ah, bl) + dot(al, bh) + dot(ah, bh)
    return dot(ah, bl) + dot(
        jnp.concatenate([ah, al], axis=1), jnp.concatenate([bh, bh], axis=0)
    )


def both(pair):
    return jnp.concatenate([pair[0], pair[1]], axis=1)


def classes(cols):
    if cols == 32:
        start_z = (0.0, 0.9, 1.9, 2.8, 5.8, 6.7, 7.6, 8.4)
        start_y = (0.4, 2.2, 4.7, 3.3)
        start = {4 * z + y: start_z[z] + start_y[y] for z in range(8) for y in range(4)}
        served = {(5, 0): (4, 0), (6, 0): (3, 0), (7, 0): (1, 0), (3, 2): (2, 2)}
        for y in (1, 2, 3):
            served.update({(4 + k, y): (3 - k, y) for k in range(4)})
        served[4, 2] = (2, 2)
        partner = {4 * a + b: 4 * d + e for (a, b), (d, e) in served.items()}
    else:
        start = {k: k for k in range(cols)}
        partner = {k: k - cols // 2 for k in range((cols + 1) // 2, cols)}
    order = sorted(start, key=lambda k: start[k])
    early = [k for k in order if k not in partner]
    return early, [k for k in order if k in partner], partner


def kernel(
    rows, cols, off_hbm, plan_hbm, e_ref, v_ref, t_ref, y_ref,
    off_ref, plan_ref, xin, xt, low, up, mine, g1, stage, g2, g3, ebuf, p1buf, fbuf, abuf, hbuf, bbuf, pbuf, sbuf, cbuf, dbuf,
    lsem, msem, hsem, s1, s2, s3, esem, psem, asem, bsend, brecv, dsem, rowsem, colsem, gosem,
):
    nb = t_ref.shape[1]
    part = nb // rows
    own = e_ref.shape[0]
    r = lax.axis_index("row")
    c = lax.axis_index("col")
    core, pair, x = r % 2, (r // 2) % 2, r // 4
    groups = rows // 4
    early, late, partner = classes(cols)
    blocks = 2 * rows - 2

    is_late = functools.reduce(jnp.logical_or, [c == k for k in late])
    server = sum(jnp.where(c == a, b, 0) for a, b in partner.items())
    is_early = jnp.logical_not(is_late)

    def row_at(k):
        return lax.rem(r + k, rows)

    swaps = cols % 8 == 0

    def across(k):
        return (lax.rem(c - k + 4 * cols, 4) == 2).astype(jnp.int32) if swaps else 0

    def row_for(k):
        return r ^ (2 * across(k))

    def remote(src, dst, send, recv, to_row, to_col):
        return pltpu.make_async_remote_copy(
            src_ref=src, dst_ref=dst, send_sem=send, recv_sem=recv,
            device_id=(to_row, to_col), device_id_type=MESH,
        )

    def signal(sem, to_row, to_col):
        pl.semaphore_signal(sem, 1, device_id=(to_row, to_col), device_id_type=MESH)

    def await_bytes(ref, sem):
        pltpu.make_async_copy(ref, ref, sem).wait()

    mine_parts = []
    for i in range(1 + swaps):
        at = pl.multiple_of((r ^ (2 * i)) * part, part)
        end = jnp.minimum(nb + at + part - 1, 2 * nb - 2)
        mine_parts += [
            pltpu.make_async_copy(v_ref.at[pl.ds(at, part), 0], low.at[i], msem.at[i, 0]),
            pltpu.make_async_copy(
                v_ref.at[pl.ds(nb + at, part - 1), 0],
                up.at[i, pl.ds(0, part - 1)],
                msem.at[i, 1],
            ),
            pltpu.make_async_copy(
                v_ref.at[pl.ds(end, 1), 0], up.at[i, pl.ds(part - 1, 1)], msem.at[i, 2]
            ),
            pltpu.make_async_copy(
                t_ref.at[0, pl.ds(at, part)], mine.at[i, pl.ds(part, part)], msem.at[i, 3]
            ),
        ]
    get_e = pltpu.make_async_copy(e_ref, xin.at[pl.ds(own, own)], lsem.at[0])
    get_plan = pltpu.make_async_copy(plan_hbm, plan_ref, lsem.at[1])
    get_off = pltpu.make_async_copy(off_hbm, off_ref, lsem.at[2])
    for copy in mine_parts:
        copy.start()

    barrier = pltpu.get_barrier_semaphore()

    @pl.when(is_early)
    def _():
        for k in late[::-1] + early[::-1]:
            @pl.when(c != k)
            def _(k=k):
                signal(barrier, row_for(k), k)
        for k in range(1, rows):
            signal(barrier, row_at(k), c)

        for a, b in partner.items():
            @pl.when(c == b)
            def _(a=a):
                for k in range(1, rows):
                    signal(barrier, row_at(k), a)

    @pl.when(is_late)
    def _():
        pl.semaphore_wait(barrier, len(early) + rows - 1)
        for k in early:
            signal(colsem, row_for(k), k)
        for k in range(1, rows):
            signal(rowsem, row_at(k), server)

    @pl.when(core == 0)
    def _():
        xin[own - nb : own] = jnp.zeros((nb, nb), F32)

    for copy in mine_parts:
        copy.wait()
    for i in range(1 + swaps):
        at = (r ^ (2 * i)) * part
        row_ids = lax.broadcasted_iota(jnp.int32, (part, nb), 0) + at
        col_ids = lax.broadcasted_iota(jnp.int32, (part, nb), 1)
        mine[i, 0:part] = jnp.where(row_ids >= col_ids, low[i], up[i])

    @pl.when(is_early)
    def _():
        pl.semaphore_wait(barrier, len(early) - 1 + rows - 1)

    def share(to):
        for k in to:
            @pl.when(c != k)
            def _(k=k):
                remote(
                    mine.at[across(k)], g1.at[c], s1.at[0], s1.at[1], row_for(k), k
                ).start()

    share(early)
    for copy in (get_e, get_plan, get_off):
        copy.start()
    head = remote(
        e_ref, xin.at[pl.ds(2 * own, own)], hsem.at[0], hsem.at[1], row_at(rows - 1), c
    )
    tail = remote(e_ref, xin.at[pl.ds(0, own)], hsem.at[2], hsem.at[3], r ^ 1, c)

    def send_rows():
        head.start()

        @pl.when(core == 0)
        def _():
            tail.start()

    got1 = g1.at[pl.ds(0, cols - 1)]
    g1[c] = mine[0]

    @pl.when(is_early)
    def _():
        send_rows()
        pl.semaphore_wait(colsem, len(late))
        for b in sorted(set(partner.values())):
            served = [k for k in late if partner[k] == b]

            @pl.when(c == b)
            def _(served=served):
                pl.semaphore_wait(rowsem, (rows - 1) * len(served))
                for a in served:
                    signal(gosem, r, a)

        share(late)

    @pl.when(is_late)
    def _():
        pl.semaphore_wait(gosem, 1)
        share(late)
        send_rows()

    await_bytes(got1, s1.at[1])
    get_plan.wait()
    get_off.wait()

    chips = rows // 2
    chip = r // 2
    core0, core1 = core == 0, core == 1
    order = sorted(range(1, chips), key=lambda k: -min(k, chips - k)) + [0]

    def wave(h):
        return pl.ds(4 * part * h, 4 * part)

    def to_chip(k, h):
        to = 2 * lax.rem(chip + k, chips) + 1
        return remote(
            stage.at[k, wave(h)], g2.at[r, wave(h)], s2.at[0, h], s2.at[1, h], to, c
        )

    for h in range(2):
        for k in order:
            for j in (2 * h, 2 * h + 1):
                block = jnp.clip(4 * lax.rem(chip + k, chips) - 1 + j, 0, blocks - 1)
                stage[k, 2 * part * j : 2 * part * (j + 1)] = g1[plan_ref[0, block]]
        for k in order[:-1]:
            to_chip(k, h).start()

        @pl.when(core0)
        def _(h=h):
            to_chip(0, h).start()

    @pl.when(core1)
    def _():
        g2[r] = stage[0]
        tail.wait_recv()

    get_e.wait()
    head.wait_recv()
    off = off_ref[0]
    s0 = xin[pl.ds(off + own - nb, nb)]

    ri = lax.broadcasted_iota(jnp.int32, (nb, nb), 0)
    ci = lax.broadcasted_iota(jnp.int32, (nb, nb), 1)
    eye = (ri == ci).astype(F32)

    def triangles(packed):
        packed = packed.reshape(nb, nb)
        return jnp.where(ri >= ci, packed, 0.0), jnp.where(ri >= ci, 0.0, packed)

    def fresh(n):
        return xin[pl.ds(off + own + nb * (n + 1), nb)]

    def entry(j):
        lo = 2 * part * j
        return g2[:, lo : lo + part], g2[:, lo + part : lo + 2 * part]

    def keep_transposed(blocks_of):
        for n in blocks_of:
            xt[n + 3] = fresh(n).T

    def live(n, factor):
        inside = ((2 * r + n >= 0) & (2 * r + n < blocks)).astype(F32)
        return factor.reshape(nb, nb) * inside

    def sides(n, lower, upper):
        return jnp.concatenate([lower, mm(xt[n + 3], upper)], axis=0)

    def passed(n, packed, factor):
        lower, upper = triangles(packed)
        w = mm(mm(upper, live(n, factor)), sides(n, lower, upper), rhs_t=True)
        return -w[:, :nb], fresh(n) - w[:, nb:]

    def done(n, packed, factor):
        lower, upper = triangles(packed)
        w = mm(mm(lower, live(n, factor)), sides(n, lower, upper), rhs_t=True)
        return eye - w[:, :nb], -w[:, nb:]

    entries = remote(
        g2.at[:, pl.ds(0, 6 * part)], g2.at[:, pl.ds(0, 6 * part)],
        esem.at[0], esem.at[1], r ^ 1, c,
    )
    third = remote(
        g2.at[:, pl.ds(0, 2 * part)], g3, s3.at[0], s3.at[1], row_at(rows - 2), c
    )
    to_pair = remote(fbuf, abuf, asem.at[0], asem.at[1], r ^ 2, c)
    prefix = remote(abuf, pbuf, psem.at[0], psem.at[1], r ^ 1, c)
    state = remote(sbuf, sbuf, dsem.at[0], dsem.at[1], r ^ 1, c)

    @pl.when(core1)
    def _():
        keep_transposed(range(-3, 2))
        await_bytes(g2.at[pl.ds(0, rows - 1), wave(0)], s2.at[1, 0])
        third.start()
        (a0, b0), (a1, b1) = [passed(j - 3, *entry(j)) for j in (0, 1)]
        first = mm(a1, jnp.concatenate([a0, b0], axis=1))
        p1buf[0] = first[:, :nb]
        p1buf[1] = first[:, nb:] + b1
        await_bytes(g2.at[pl.ds(0, rows - 1), wave(1)], s2.at[1, 1])
        (a2, b2), (a3, b3) = [passed(j - 3, *entry(j)) for j in (2, 3)]
        second = mm(a3, jnp.concatenate([a2, b2], axis=1))
        ebuf[0] = second[:, :nb]
        ebuf[1] = second[:, nb:] + b3
        w = mm(ebuf[0], both(p1buf))
        fbuf[0] = w[:, :nb]
        fbuf[1] = w[:, nb:] + ebuf[1]
        to_pair.start()
        entries.start()
        c2, d2 = done(-1, *entry(2))
        cbuf[0:nb] = c2
        dbuf[0:nb] = d2
        c3, d3 = done(0, *entry(3))
        w = mm(c3, jnp.concatenate([a2, b2], axis=1))
        cbuf[nb : 2 * nb] = w[:, :nb]
        dbuf[nb : 2 * nb] = w[:, nb:] + d3

    @pl.when(core0)
    def _():
        keep_transposed(range(-1, 2))
        await_bytes(g2.at[:, pl.ds(0, 6 * part)], esem.at[1])
        (a0, b0), (a1, b1) = [passed(j - 1, *entry(j)) for j in range(2)]
        (c0, d0), (c1, d1), (c2, d2) = [done(j - 1, *entry(j)) for j in range(3)]
        cbuf[0:nb] = c0
        dbuf[0:nb] = d0
        w = mm(jnp.concatenate([a1, c1], axis=0), jnp.concatenate([a0, b0], axis=1))
        cbuf[nb : 2 * nb] = w[nb:, :nb]
        dbuf[nb : 2 * nb] = w[nb:, nb:] + d1
        g, b = w[:nb, :nb], w[:nb, nb:] + b1
        w = mm(c2, jnp.concatenate([g, b], axis=1))
        cbuf[2 * nb : 3 * nb] = w[:, :nb]
        dbuf[2 * nb : 3 * nb] = w[:, nb:] + d2

    def along_x(step, whole):
        src, dst = (hbuf, bbuf.at[x]) if whole else (hbuf.at[1], bbuf.at[x, 1])
        return remote(
            src, dst, bsend.at[step, 0], brecv.at[x, 0], lax.rem(r + 4 * step, rows), c
        )

    @pl.when(core1)
    def _():
        to_pair.wait_recv()
        first = pair == 0

        @pl.when(pair == 1)
        def _():
            prefix.start()

        late_g = jnp.where(first, abuf[0], fbuf[0])
        late_b = jnp.where(first, abuf[1], fbuf[1])
        early_pair = jnp.where(first, both(fbuf), both(abuf))
        w = mm(late_g, early_pair)
        hbuf[0] = w[:, :nb]
        hbuf[1] = w[:, nb:] + late_b
        for step in range(groups - 1, 0, -1):
            @pl.when(x + step < groups)
            def _(step=step):
                @pl.when(x == 0)
                def _():
                    along_x(step, False).start()

                @pl.when(x > 0)
                def _():
                    along_x(step, True).start()

    @pl.when(core1)
    def _():
        third.wait_recv()
        c4, d4 = done(1, g3[:, 0:part], g3[:, part : 2 * part])
        w = mm(c4, both(ebuf))
        cbuf[2 * nb : 3 * nb] = w[:, :nb]
        dbuf[2 * nb : 3 * nb] = w[:, nb:] + d4

    @pl.when(core1 & (pair == 0))
    def _():
        pbuf[...] = p1buf[...]

    @pl.when(core1 & (pair == 1))
    def _():
        w = mm(p1buf[0], both(abuf))
        pbuf[0] = w[:, :nb]
        pbuf[1] = w[:, nb:] + p1buf[1]

    @pl.when(core0 & (pair == 1))
    def _():
        prefix.wait_recv()

    @pl.when(core1 | (pair == 1))
    def _():
        w = mm(cbuf[...], both(pbuf))
        cbuf[...] = w[:, :nb]
        dbuf[...] = w[:, nb:] + dbuf[...]

    @pl.when(x == 0)
    def _():
        sbuf[...] = s0

    @pl.when((x > 0) & core1)
    def _():
        for source in range(groups - 1):
            @pl.when(x > source)
            def _(source=source):
                await_bytes(bbuf.at[source] if source else bbuf.at[0, 1], brecv.at[source, 0])
                if source:
                    sbuf[...] = mm(bbuf[source, 0], sbuf[...]) + bbuf[source, 1]
                else:
                    sbuf[...] = bbuf[source, 1]
        state.start()

    @pl.when((x > 0) & core0)
    def _():
        state.wait_recv()

    dbuf[...] = mm(cbuf[...], sbuf[...]) + dbuf[...]
    y_ref[...] = dbuf[pl.ds(nb - off, own)]

    await_bytes(got1, s1.at[0])
    head.wait_send()
    for h in range(2):
        await_bytes(stage.at[pl.ds(0, chips - 1), wave(h)], s2.at[0, h])

    @pl.when(core0)
    def _():
        for h in range(2):
            await_bytes(stage.at[0, wave(h)], s2.at[0, h])
        tail.wait_send()

    @pl.when(core1)
    def _():
        entries.wait_send()
        third.wait_send()
        to_pair.wait_send()

        @pl.when(pair == 1)
        def _():
            prefix.wait_send()

        @pl.when(x > 0)
        def _():
            state.wait_send()

        for step in range(1, groups):
            @pl.when(x + step < groups)
            def _(step=step):
                @pl.when(x == 0)
                def _():
                    along_x(step, False).wait_send()

                @pl.when(x > 0)
                def _():
                    along_x(step, True).wait_send()


def solution(mesh):
    rows, cols = mesh.shape["row"], mesh.shape["col"]

    def on_device(eigvecs, offsets, plan, refl_v, refl_t):
        own, width = eigvecs.shape
        nb = refl_t.shape[1]
        part = nb // rows
        dma = pltpu.SemaphoreType.DMA
        square = (nb, nb)
        y = pl.pallas_call(
            functools.partial(kernel, rows, cols),
            out_shape=pltpu.VMEM((own, width), F32),
            in_specs=[
                pl.BlockSpec(memory_space=pl.ANY),
                pl.BlockSpec(memory_space=pl.ANY),
                pl.BlockSpec(memory_space=pl.ANY),
                pl.BlockSpec(memory_space=pl.ANY),
                pl.BlockSpec(memory_space=pl.ANY),
            ],
            out_specs=pl.BlockSpec(memory_space=pltpu.VMEM),
            scratch_shapes=[
                pltpu.SMEM(offsets.shape, jnp.int32),
                pltpu.SMEM(plan.shape, jnp.int32),
                pltpu.VMEM((3 * own, width), F32),
                pltpu.VMEM((5, nb, width), F32),
                pltpu.VMEM((2, part, nb), F32),
                pltpu.VMEM((2, part, nb), F32),
                pltpu.VMEM((2, 2 * part, nb), F32),
                pltpu.VMEM((cols, 2 * part, nb), F32),
                pltpu.VMEM((rows // 2, 8 * part, nb), F32),
                pltpu.VMEM((rows, 8 * part, nb), F32),
                pltpu.VMEM((rows, 2 * part, nb), F32),
                pltpu.VMEM((2,) + square, F32),
                pltpu.VMEM((2,) + square, F32),
                pltpu.VMEM((2,) + square, F32),
                pltpu.VMEM((2,) + square, F32),
                pltpu.VMEM((2,) + square, F32),
                pltpu.VMEM((rows // 4, 2) + square, F32),
                pltpu.VMEM((2,) + square, F32),
                pltpu.VMEM(square, F32),
                pltpu.VMEM((3 * nb, nb), F32),
                pltpu.VMEM((3 * nb, width), F32),
                dma((3,)), dma((2, 4)), dma((4,)), dma((2,)), dma((2, 2)), dma((2,)), dma((2,)), dma((2,)), dma((2,)),
                dma((rows // 4, 2)), dma((rows // 4, 2)), dma((2,)),
                pltpu.SemaphoreType.REGULAR, pltpu.SemaphoreType.REGULAR,
                pltpu.SemaphoreType.REGULAR,
            ],
            compiler_params=pltpu.CompilerParams(
                collective_id=0, has_side_effects=True, vmem_limit_bytes=60 * 2**20
            ),
            cost_estimate=pl.CostEstimate(
                flops=2 * 30 * nb**3, bytes_accessed=4 * 10 * nb * nb, transcendentals=0
            ),
            name="chase",
        )(offsets, plan, eigvecs, refl_v.transpose(1, 0, 2), refl_t)
        return y

    return jax.shard_map(
        on_device,
        mesh=mesh,
        in_specs=(P("row", "col"), P(), P(), P("col", None, None), P("col", None, None)),
        out_specs=P("row", "col"),
        check_vma=False,
    )
```
